32 devices in a mesh: groups: 2 (over y), src: 4 (over z), tgt: 2 (over x), dir: 2 (over core).
Axes of the slice: x: 2, y: 2, z: 4, core: 2. Of those that a mesh axis runs over, the one named last changes fastest.
Arguments:
- incident: bfloat16 [2, 64, 4096], P(None, 'dir', ('groups', 'src')), parts along dimension 2, may hold values from -6 to 6
- near_blocks: bfloat16 [8, 2, 56, 2, 128, 128], P(('groups', 'src'), 'tgt'), parts along dimension 0, may hold values from -0.25 to 0.25
- near_src: int32 [8, 2, 56], P(('groups', 'src'), 'tgt'), parts along dimension 0, may hold values from 0 to 3
- near_tgt: int32 [8, 2, 56], P(('groups', 'src'), 'tgt'), parts along dimension 0, may hold values from 0 to 15, as said below
- far_v: bfloat16 [8, 2, 32, 2, 32, 128], P(('groups', 'src'), 'tgt'), parts along dimension 0, may hold values from -0.5 to 0.5
- far_src: int32 [8, 2, 32], P(('groups', 'src'), 'tgt'), parts along dimension 0, may hold values from 0 to 3
- far_dst: int32 [8, 2, 32], P(('groups', 'src'), 'tgt'), parts along dimension 0, may hold values from 0 to 127, as said below
- far_u: bfloat16 [8, 2, 32, 2, 32, 128], P(('groups', 'src'), 'tgt'), parts along dimension 0, may hold values from -0.75 to 0.75
- far_tgt: int32 [8, 2, 32], P(('groups', 'src'), 'tgt'), parts along dimension 0, may hold values from 0 to 3
Outputs:
- potential: float32 [2, 64, 4096], P(None, 'dir', ('groups', 'src', 'tgt')), parts along dimension 2
The draws below stay inside these ranges and needn't reach their ends.
There are 2 independent parts, one for each index of `groups`. The reference program is written for one: setup_inputs(seed, part) draws one part's arguments, and reference() takes and returns one part's arrays. A program takes and returns all parts, laid end to end along the dimension named above; each array names one. Nothing has to cross between parts.
Inputs may be any that keep to these rules, and one draw needn't show every extreme that they name: Near block (s, t, b) aims at owner near_tgt // 4. The near blocks of one device aimed at one owner other than s number at most 2 and reach at most 1 distinct target cluster; in every draw some owner receives exactly 2 near blocks from every device of every other owner. `far_dst`: value v names owner v // 32 and slot v % 32 at the same tgt index. Among the devices of one tgt index every value occurs exactly once; one device sends exactly 8 far blocks or none to each owner.
All inputs are finite; a program needn't handle non-finite values.
Results may differ from the reference program's by a relative error of at most 0.0025.
Values may be sent and summed in bfloat16 or wider, within the bound.
No kernel may reach another device: no remote copies, remote signals or barrier semaphores. Data moves between devices by JAX's collectives and lax.ppermute only.
A program may use at most 64 MiB of HBM per device.

```python
import jax
import jax.numpy as jnp
from jax import lax

DIRS = 64
PANEL = 128
RANK = 32
NB_DEV = 56
FB_DEV = 32
CAP = 2
OWNERS = 4
QUARTERS = 2
CL_SRC = 4
CLUSTERS = 16
PANELS = 2048
CAPF = 8


def draw_near_tgt(key, part):
    hot_key, pool_key, order_key, contact_key, anywhere_key = jax.random.split(jax.random.fold_in(key, 11), 5)
    hot_owner = jax.random.randint(hot_key, (), 0, OWNERS)
    owner_ids = jnp.arange(OWNERS, dtype=jnp.int32)[:, None, None]
    hot_for = jnp.where(owner_ids == hot_owner, (hot_owner + 1) % OWNERS, hot_owner)
    width = NB_DEV + OWNERS * CAP
    self_part = jnp.broadcast_to(owner_ids, (OWNERS, QUARTERS, NB_DEV))
    other_part = jnp.broadcast_to((jnp.arange(OWNERS * CAP, dtype=jnp.int32) // CAP)[None, None, :], (OWNERS, QUARTERS, OWNERS * CAP))
    candidates = jnp.concatenate([self_part, other_part], axis=2)
    other_ok = (other_part != owner_ids) & (other_part != hot_for)
    usable = jnp.concatenate([jnp.ones((OWNERS, QUARTERS, NB_DEV), dtype=bool), other_ok], axis=2)
    position = jnp.arange(width, dtype=jnp.int32)[None, None, :]
    scores = jax.random.randint(pool_key, (OWNERS, QUARTERS, width), 0, 2 ** 20) * width + position
    scores = jnp.where(usable, scores, 2 ** 20 * width + position)
    taken = jnp.argsort(scores, axis=2)[:, :, :NB_DEV - CAP]
    picked = jnp.take_along_axis(candidates, taken, axis=2)
    destination = jnp.concatenate([jnp.broadcast_to(hot_for, (OWNERS, QUARTERS, CAP)), picked], axis=2)
    shuffle = jnp.argsort(jax.random.randint(order_key, (OWNERS, QUARTERS, NB_DEV), 0, 2 ** 20) * NB_DEV + jnp.arange(NB_DEV, dtype=jnp.int32)[None, None, :], axis=2)
    destination = jnp.take_along_axis(destination, shuffle, axis=2)
    contact = jax.random.randint(contact_key, (OWNERS, QUARTERS, OWNERS), 0, CL_SRC)
    aimed_at = jnp.take_along_axis(contact, destination, axis=2)
    anywhere = jax.random.randint(anywhere_key, (OWNERS, QUARTERS, NB_DEV), 0, CL_SRC)
    cluster = jnp.where(destination == owner_ids, anywhere, aimed_at)
    return (destination * CL_SRC + cluster).astype(jnp.int32)


def draw_far_dst(key, part):
    route_key, slot_key, order_key = jax.random.split(jax.random.fold_in(key, 23), 3)
    routes = jax.vmap(lambda sub_key: jax.random.permutation(sub_key, OWNERS))(jax.random.split(route_key, QUARTERS))
    slot_perm = jax.vmap(lambda sub_key: jax.random.permutation(sub_key, FB_DEV))(jax.random.split(slot_key, OWNERS * QUARTERS))
    slot_perm = slot_perm.reshape(OWNERS, QUARTERS, FB_DEV)
    owner_ids = jnp.arange(OWNERS, dtype=jnp.int32)[:, None, None]
    quarter_ids = jnp.arange(QUARTERS, dtype=jnp.int32)[None, :, None]
    item_ids = jnp.arange(FB_DEV, dtype=jnp.int32)[None, None, :]
    owner_of = routes[quarter_ids, (owner_ids + item_ids // CAPF) % OWNERS]
    encoded = owner_of * FB_DEV + slot_perm[owner_of, quarter_ids, item_ids]
    reorder = jnp.argsort(jax.random.randint(order_key, (OWNERS, QUARTERS, FB_DEV), 0, 2 ** 20) * FB_DEV + item_ids, axis=2)
    return jnp.take_along_axis(encoded, reorder, axis=2).astype(jnp.int32)


def plant(drawn, stream_key, low, largest):
    dims = drawn.shape
    spot = [jax.random.randint(jax.random.fold_in(stream_key, axis), (), 0, dims[axis]) for axis in range(len(dims))]
    drawn = drawn.at[tuple(spot)].set(low)
    longest = dims.index(max(dims))
    spot[longest] = (spot[longest] + 1) % dims[longest]
    return drawn.at[tuple(spot)].set(largest)


def steps_of(key, extent, shards, smallest, high):
    factor_of, own = 1.0, jax.random.fold_in(key, 6)
    for axis_at, parts in shards:
        draws = jnp.exp(jax.random.uniform(jax.random.fold_in(own, axis_at), (parts,), jnp.float32, smallest / len(shards), high / len(shards)))
        factor_of = factor_of * jnp.repeat(draws, extent[axis_at] // parts).reshape([-1 if axis == axis_at else 1 for axis in range(len(extent))])
    return factor_of


def centred(own_key, extent, spread, bound, cuts=(), held_as=jnp.bfloat16):
    array = spread * jax.random.normal(own_key, extent, jnp.float32)
    if cuts:
        array = array * steps_of(own_key, extent, cuts, -0.22, 0.18)
    return jnp.clip(array, -bound, bound).astype(held_as)


def setup_inputs(seed: int = 0, part: int = 0) -> dict:
    key_of = jax.random.split(jax.random.key(seed), 10)
    part_splits = jax.random.split(jax.random.fold_in(key_of[9], part), 10)
    return {
        "incident": centred(part_splits[0], (2, DIRS, PANELS), 1.0, 6.0, ((1, 2), (2, 4))),
        "near_blocks": centred(part_splits[1], (OWNERS, QUARTERS, NB_DEV, 2, PANEL, PANEL), (4 * PANEL) ** -0.5, 0.25, ((0, 4), (1, 2))),
        "near_src": plant(jax.random.randint(part_splits[2], (OWNERS, QUARTERS, NB_DEV), 0, CL_SRC), jax.random.fold_in(part_splits[2], 1), 0, CL_SRC - 1).astype(jnp.int32),
        "near_tgt": draw_near_tgt(jax.random.fold_in(jax.random.fold_in(key_of[9], part), 71), part),
        "far_v": centred(part_splits[4], (OWNERS, QUARTERS, FB_DEV, 2, RANK, PANEL), PANEL ** -0.5, 0.5, ((0, 4), (1, 2))),
        "far_src": plant(jax.random.randint(part_splits[5], (OWNERS, QUARTERS, FB_DEV), 0, CL_SRC), jax.random.fold_in(part_splits[5], 1), 0, CL_SRC - 1).astype(jnp.int32),
        "far_dst": draw_far_dst(jax.random.fold_in(jax.random.fold_in(key_of[9], part), 71), part),
        "far_u": centred(part_splits[7], (OWNERS, QUARTERS, FB_DEV, 2, RANK, PANEL), (2 * RANK) ** -0.5, 0.75, ((0, 4), (1, 2))),
        "far_tgt": plant(jax.random.randint(part_splits[8], (OWNERS, QUARTERS, FB_DEV), 0, CL_SRC), jax.random.fold_in(part_splits[8], 1), 0, CL_SRC - 1).astype(jnp.int32),
    }


def complex_apply(operand, matrices, pattern):
    products = jnp.einsum(pattern, operand.astype(jnp.float32), matrices.astype(jnp.float32), precision=lax.Precision.HIGHEST)
    return jnp.stack([products[:, 0, 0] - products[:, 1, 1], products[:, 1, 0] + products[:, 0, 1]], axis=1)


def reference(incident, near_blocks, near_src, near_tgt, far_v, far_src, far_dst, far_u, far_tgt):
    source = incident.reshape(2, DIRS, OWNERS, CL_SRC, PANEL)
    owner_ids = jnp.arange(OWNERS, dtype=jnp.int32)

    def near_step(cluster_total, owner_index):
        blocks = near_blocks[owner_index].reshape(QUARTERS * NB_DEV, 2, PANEL, PANEL)
        picked = jnp.take(source[:, :, owner_index], near_src[owner_index].reshape(-1).astype(jnp.int32), axis=2)
        partial_value = complex_apply(picked, blocks, "adbq,bcpq->bacdp")
        return cluster_total.at[near_tgt[owner_index].reshape(-1).astype(jnp.int32)].add(partial_value), None

    cluster_total = jnp.zeros((CLUSTERS, 2, DIRS, PANEL), jnp.float32)
    cluster_total, unused_near = lax.scan(near_step, cluster_total, owner_ids)

    def coeff_step(carried, owner_index):
        picked = jnp.take(source[:, :, owner_index], far_src[owner_index].reshape(-1).astype(jnp.int32), axis=2)
        factors = far_v[owner_index].reshape(QUARTERS * FB_DEV, 2, RANK, PANEL)
        coeffs = complex_apply(picked, factors, "adbq,bckq->bacdk").astype(jnp.bfloat16)
        return carried, coeffs.reshape(QUARTERS, FB_DEV, 2, DIRS, RANK)

    unused_carry, coefficients = lax.scan(coeff_step, jnp.zeros((), jnp.float32), owner_ids)
    quarter_ids = jnp.broadcast_to(jnp.arange(QUARTERS, dtype=jnp.int32)[None, :, None], far_dst.shape)
    arranged = jnp.zeros((QUARTERS, OWNERS * FB_DEV, 2, DIRS, RANK), coefficients.dtype)
    arranged = arranged.at[quarter_ids, far_dst.astype(jnp.int32)].set(coefficients)
    arranged = arranged.reshape(QUARTERS, OWNERS, FB_DEV, 2, DIRS, RANK).transpose(1, 0, 2, 3, 4, 5)

    def far_step(cluster_total, owner_index):
        factors = far_u[owner_index].reshape(QUARTERS * FB_DEV, 2, RANK, PANEL)
        coeffs = arranged[owner_index].reshape(QUARTERS * FB_DEV, 2, DIRS, RANK)
        potential = complex_apply(coeffs, factors, "badk,bckp->bacdp")
        clusters = owner_index * CL_SRC + far_tgt[owner_index].reshape(-1).astype(jnp.int32)
        return cluster_total.at[clusters].add(potential), None

    cluster_total, unused_far = lax.scan(far_step, cluster_total, owner_ids)
    return cluster_total.transpose(1, 2, 0, 3).reshape(2, DIRS, PANELS)
```

```python
import functools

import jax
import jax.numpy as jnp
from jax import lax
from jax.experimental import pallas as pl
from jax.experimental.pallas import tpu as pltpu
from jax.sharding import PartitionSpec as P

PANEL = 128
LANES = 128
LABEL_ROWS = 16
LIMIT = 24 << 20
VMEM = pl.BlockSpec(memory_space=pltpu.VMEM)
SMEM = pl.BlockSpec(memory_space=pltpu.SMEM)
PARAMS = pltpu.CompilerParams(vmem_limit_bytes=LIMIT)


def div_by(value, size):
    if size & (size - 1) == 0:
        return lax.shift_right_logical(value, jnp.int32(size.bit_length() - 1))
    return lax.div(value, jnp.int32(size))


def ahead_of(owner, me, owners):
    ahead = owner - me
    return jnp.where(ahead < 0, ahead + owners, ahead)


def dot_nt(left, right):
    return lax.dot_general(left, right, (((1,), (1,)), ((), ())), preferred_element_type=jnp.float32)


def dot_nn(left, right):
    return jnp.dot(left, right, preferred_element_type=jnp.float32)


def coeff_kernel(owners, depth, far_src, far_dst, incident, far_v, field, labels, *rest):
    outs, (ordered, source_of) = rest[:owners], rest[owners:]
    me = lax.axis_index("src")
    clusters = incident.shape[2] // PANEL
    half = incident.shape[1]
    rows = 2 * half
    blocks, rank = far_v.shape[2], far_v.shape[4]
    per_chunk = LANES // rank
    lane = lax.broadcasted_iota(jnp.int32, (1, LANES), 1)
    for s in range(clusters):
        real, imag = (incident[c, :, s * PANEL:(s + 1) * PANEL] for c in range(2))
        field[s * rows:s * rows + half, :] = jnp.concatenate([real, -imag], axis=1)
        field[s * rows + half:(s + 1) * rows, :] = jnp.concatenate([imag, real], axis=1)
    if owners * depth != blocks:
        ordered[...] = jnp.zeros_like(ordered)
        for place in range(owners * depth):
            source_of[place] = 0
    counts = [jnp.int32(0)] * owners
    label_row = jnp.full((1, LANES), -1, jnp.int32)
    for f in range(blocks):
        routed = far_dst[0, 0, f]
        owner = div_by(routed, blocks)
        slot = routed - owner * blocks
        ahead = ahead_of(owner, me, owners)
        taken = jnp.int32(0)
        for k in range(owners):
            taken = jnp.where(ahead == k, counts[k], taken)
            counts[k] = jnp.where(ahead == k, counts[k] + 1, counts[k])
        place = ahead * depth + taken
        at = pl.ds(pl.multiple_of(place * rank, rank), rank)
        ordered[at, 0:PANEL] = far_v[0, 0, f, 0]
        ordered[at, PANEL:2 * PANEL] = far_v[0, 0, f, 1]
        source_of[place] = far_src[0, 0, f]
        label_row = jnp.where(lane == place, slot, label_row)
    labels[...] = jnp.broadcast_to(label_row, (8, LANES))
    group = lane // rank
    everything = field[...]
    for chunk in range(owners * depth // per_chunk):
        source = jnp.zeros((1, LANES), jnp.int32)
        for at in range(per_chunk):
            source = jnp.where(group == at, source_of[chunk * per_chunk + at], source)
        product = dot_nt(everything, ordered[chunk * LANES:(chunk + 1) * LANES, :])
        chosen = product[0:rows]
        for s in range(1, clusters):
            chosen = jnp.where(source == s, product[s * rows:(s + 1) * rows], chosen)
        chunks = depth // per_chunk
        at = chunk % chunks
        outs[chunk // chunks][at * rows:(at + 1) * rows, :] = chosen.astype(jnp.bfloat16)


def near_out_kernel(owners, near_src, near_tgt, near_row, field, labels, near_blocks, *rest):
    coeffs, outs = rest[:owners - 1], rest[owners - 1:]
    me = lax.axis_index("src")
    rows = outs[0].shape[0] - LABEL_ROWS - coeffs[0].shape[0]
    clusters = field.shape[0] // rows
    count = near_row.shape[2]
    targets = near_row[0]
    position = lax.broadcasted_iota(jnp.int32, targets.shape, 1)
    lane = lax.broadcasted_iota(jnp.int32, (1, LANES), 1)
    near_labels = jnp.full((1, LANES), -1, jnp.int32)
    for k in range(1, owners):
        owner = me + k
        owner = jnp.where(owner >= owners, owner - owners, owner)
        low = owner * clusters
        aimed = (targets >= low) & (targets < low + clusters)
        first = jnp.min(jnp.where(aimed, position, count))
        last = jnp.max(jnp.where(aimed, position, -1))
        filled = last >= 0
        first = jnp.minimum(first, count - 1)
        final = jnp.maximum(last, 0)
        cluster = jnp.where(filled, near_tgt[0, 0, first] - low, -1)
        near_labels = jnp.where(lane == k, cluster, near_labels)
        total = None
        for at, used in ((first, filled), (final, last > first)):
            source = pl.ds(pl.multiple_of(near_src[0, 0, at] * rows, rows), rows)
            matrix = jnp.concatenate([near_blocks[0, 0, at, 0], near_blocks[0, 0, at, 1]], axis=1)
            part = jnp.where(used, dot_nt(field[source, :], matrix), 0.0)
            total = part if total is None else total + part
        depth_rows = coeffs[k - 1].shape[0]
        outs[k - 1][0:depth_rows, :] = coeffs[k - 1][...]
        outs[k - 1][depth_rows:depth_rows + rows, :] = total.astype(jnp.bfloat16)
    far_part = labels[0:8, :].astype(jnp.float32)
    near_part = jnp.broadcast_to(near_labels, (8, LANES)).astype(jnp.float32)
    label_tile = jnp.concatenate([far_part, near_part], axis=0).astype(jnp.bfloat16)
    for k in range(1, owners):
        outs[k - 1][outs[k - 1].shape[0] - LABEL_ROWS:, :] = label_tile


def near_own_kernel(near_src, near_tgt, field, near_blocks, total):
    me = lax.axis_index("src")
    clusters = total.shape[0] - 1
    rows = total.shape[1]
    total[...] = jnp.zeros_like(total)
    for b in range(near_blocks.shape[2]):
        target = near_tgt[0, 0, b] - me * clusters
        target = jnp.where((target >= 0) & (target < clusters), target, clusters)
        source = pl.ds(pl.multiple_of(near_src[0, 0, b] * rows, rows), rows)
        matrix = jnp.concatenate([near_blocks[0, 0, b, 0], near_blocks[0, 0, b, 1]], axis=1)
        total[target] += dot_nt(field[source, :], matrix)


def pick(vector, where):
    return jnp.sum(jnp.where(where, vector, 0))


def target_kernel(owners, depth, used, sharers, steps, far_tgt, labels, own_coeffs, far_u, total, *rest):
    messages = rest[:owners - 1]
    outs = rest[owners - 1:owners - 1 + len(steps)]
    right = rest[owners - 1 + len(steps)]
    clusters = total.shape[0] - 1
    rows = total.shape[1]
    half = rows // 2
    share = clusters // sharers
    blocks, rank = far_u.shape[2], far_u.shape[4]
    chunks = depth * rank // LANES
    me = lax.axis_index("tgt")
    lane = lax.broadcasted_iota(jnp.int32, (1, LANES), 1)
    bases = []
    for step in steps:
        holder = me + step
        holder = jnp.where(holder >= sharers, holder - sharers, holder)
        bases.append(holder * share)
    width = share * PANEL
    sums = [jnp.concatenate([total[base + c] for c in range(share)], axis=1) for base in bases]
    for k in range(owners):
        if k == 0:
            far_labels = labels[0:1, :]
            coeffs = own_coeffs
        else:
            message = messages[k - 1]
            tile = message[message.shape[0] - LABEL_ROWS:, :].astype(jnp.float32)
            far_labels = tile[0:1].astype(jnp.int32)
            near_label = pick(tile[8:9].astype(jnp.int32), lane == k)
            coeffs = message
            near = message[chunks * rows:(chunks + 1) * rows, :].astype(jnp.float32)
            for i, base in enumerate(bases):
                sums[i] = sums[i] + jnp.concatenate(
                    [jnp.where(near_label == base + c, near, 0.0) for c in range(share)], axis=1)
        values = jnp.concatenate([coeffs[c * rows:(c + 1) * rows, :] for c in range(chunks)], axis=1)
        crossed = jnp.concatenate([-values[half:rows], values[0:half]], axis=0)
        spread = depth * rank
        for r in range(depth):
            if r < used:
                slot = pick(far_labels, lane == k * depth + r)
                known = slot >= 0
                slot = jnp.maximum(slot, 0)
                cluster = jnp.where(known, far_tgt[0, 0, slot], -1)
            for part in range(2):
                at = (k * 2 + part) * spread + r * rank
                for i, base in enumerate(bases):
                    for c in range(share):
                        to = i * width + c * PANEL
                        if r < used:
                            factor = far_u[0, 0, slot, part]
                            factor = jnp.where(cluster == base + c, factor, jnp.zeros_like(factor))
                        else:
                            factor = jnp.zeros((rank, PANEL), jnp.bfloat16)
                        right[at:at + rank, to:to + PANEL] = factor
        for part, left in enumerate((values, crossed)):
            at = (k * 2 + part) * spread
            product = dot_nn(left, right[at:at + spread, :])
            for i in range(len(bases)):
                sums[i] = sums[i] + product[:, i * width:(i + 1) * width]
    for i, out in enumerate(outs):
        out[...] = sums[i].astype(out.dtype).reshape(out.shape)


def body(incident, near_blocks, near_src, near_tgt, far_v, far_src, far_dst, far_u, far_tgt):
    owners = lax.axis_size("src")
    sharers = lax.axis_size("tgt")
    half = incident.shape[1]
    rows = 2 * half
    clusters = incident.shape[2] // PANEL
    share = clusters // sharers
    blocks, rank = far_v.shape[2], far_v.shape[4]
    used = max(2, blocks // owners)
    per_chunk = LANES // rank
    depth = -(-used // per_chunk) * per_chunk
    chunks = depth // per_chunk
    bf16, f32, i32 = jnp.bfloat16, jnp.float32, jnp.int32

    def shape(dims, dtype):
        return jax.ShapeDtypeStruct(dims, dtype)

    field, labels, *coeffs = pl.pallas_call(
        functools.partial(coeff_kernel, owners, depth),
        out_shape=[shape((clusters * rows, 2 * PANEL), bf16), shape((8, LANES), i32)]
        + [shape((chunks * rows, LANES), bf16)] * owners,
        in_specs=[SMEM, SMEM, VMEM, VMEM],
        out_specs=[VMEM] * (2 + owners),
        scratch_shapes=[
            pltpu.VMEM((owners * depth * rank, 2 * PANEL), bf16),
            pltpu.SMEM((owners * depth,), i32),
        ],
        compiler_params=PARAMS,
        name="coefficients",
    )(far_src, far_dst, incident, far_v)
    messages = pl.pallas_call(
        functools.partial(near_out_kernel, owners),
        out_shape=[shape(((chunks + 1) * rows + LABEL_ROWS, LANES), bf16)] * (owners - 1),
        in_specs=[SMEM, SMEM] + [VMEM] * (3 + owners),
        out_specs=[VMEM] * (owners - 1),
        compiler_params=PARAMS,
        name="near_out",
    )(near_src, near_tgt, near_tgt, field, labels, near_blocks, *coeffs[1:])
    arrived = [
        lax.ppermute(message, "src", [(s, (s + k) % owners) for s in range(owners)])
        for k, message in enumerate(messages, 1)
    ]
    total = pl.pallas_call(
        near_own_kernel,
        out_shape=shape((clusters + 1, rows, PANEL), f32),
        in_specs=[SMEM, SMEM, VMEM, VMEM],
        out_specs=VMEM,
        compiler_params=PARAMS,
        cost_estimate=pl.CostEstimate(flops=2 * 56 * 256 * 128 * 64 * 8, bytes_accessed=4 << 20, transcendentals=0),
        name="near_own",
    )(near_src, near_tgt, field, near_blocks)

    def target(steps, dtype, dims):
        return pl.pallas_call(
            functools.partial(target_kernel, owners, depth, used, sharers, steps),
            out_shape=[shape(dims, dtype)] * len(steps),
            in_specs=[SMEM] + [VMEM] * (4 + owners - 1),
            out_specs=[VMEM] * len(steps),
            scratch_shapes=[pltpu.VMEM((owners * 2 * depth * rank, len(steps) * share * PANEL), bf16)],
            compiler_params=PARAMS,
            name="target_other" if steps[0] else "target_mine",
        )(far_tgt, labels, coeffs[0], far_u, total, *arrived)

    result = None
    if sharers > 1:
        others = target(tuple(range(1, sharers)), bf16, (rows, share * PANEL))
        received = [
            lax.ppermute(other, "tgt", [(t, (t + k) % sharers) for t in range(sharers)])
            for k, other in enumerate(others, 1)
        ]
    else:
        received = []
    (result,) = target((0,), f32, (2, half, share * PANEL))
    for other in received:
        result = result + other.astype(f32).reshape(result.shape)
    return result


def solution(mesh):
    placed = (
        P(None, "dir", ("groups", "src")),
        P(("groups", "src"), "tgt", None, None, None, None),
        P(("groups", "src"), "tgt", None),
        P(("groups", "src"), "tgt", None),
        P(("groups", "src"), "tgt", None, None, None, None),
        P(("groups", "src"), "tgt", None),
        P(("groups", "src"), "tgt", None),
        P(("groups", "src"), "tgt", None, None, None, None),
        P(("groups", "src"), "tgt", None),
    )
    return jax.shard_map(
        body,
        mesh=mesh,
        in_specs=placed,
        out_specs=P(None, "dir", ("groups", "src", "tgt")),
        check_vma=False,
    )
```

```python
import functools

import jax
import jax.numpy as jnp
from jax import lax
from jax.experimental import pallas as pl
from jax.experimental.pallas import tpu as pltpu
from jax.sharding import PartitionSpec as P

PANEL = 128
LANES = 128
LABEL_ROWS = 16
PACK = 4
BASE = 64
LIMIT = 24 << 20
VMEM = pl.BlockSpec(memory_space=pltpu.VMEM)
SMEM = pl.BlockSpec(memory_space=pltpu.SMEM)
HBM = pl.BlockSpec(memory_space=pltpu.HBM)
PARAMS = pltpu.CompilerParams(vmem_limit_bytes=LIMIT)


def div_by(value, size):
    if size & (size - 1) == 0:
        return lax.shift_right_logical(value, jnp.int32(size.bit_length() - 1))
    return lax.div(value, jnp.int32(size))


def wrap(value, size):
    if size & (size - 1) == 0:
        return value & (size - 1)
    return jnp.where(value < 0, value + size, jnp.where(value >= size, value - size, value))


def dot_nt(left, right):
    return lax.dot_general(left, right, (((1,), (1,)), ((), ())), preferred_element_type=jnp.float32)


def dot_nn(left, right):
    return jnp.dot(left, right, preferred_element_type=jnp.float32)


def send_kernel(owners, depth, far_src, far_dst, near_src, near_tgt, incident, far_v, near_blocks,
                field, labels, own_coeffs, *rest):
    messages, rest = rest[:owners - 1], rest[owners - 1:]
    (src_f, dst_f, src_n, tgt_n, tgt_row, waves, factors, picked, ordered, source_of, counts,
     sems, pick_sems) = rest
    me = lax.axis_index("src")
    half = waves.shape[1]
    rows = 2 * half
    clusters = waves.shape[2] // PANEL
    blocks, rank = factors.shape[2], factors.shape[4]
    count = tgt_row.shape[2]
    per_chunk = LANES // rank
    chunks = depth // per_chunk
    lane = lax.broadcasted_iota(jnp.int32, (1, LANES), 1)

    loads = [
        pltpu.make_async_copy(a, b, sems.at[i])
        for i, (a, b) in enumerate((
            (near_tgt, tgt_row), (near_tgt, tgt_n), (near_src, src_n), (far_dst, dst_f), (far_src, src_f),
            (incident, waves), (far_v, factors)))
    ]
    for load in loads:
        load.start()
    row_in, tgt_in, near_in, dst_in, far_in, waves_in, factors_in = loads

    row_in.wait()
    targets = tgt_row[0]
    position = lax.broadcasted_iota(jnp.int32, targets.shape, 1)
    chosen_near = []
    for k in range(1, owners):
        low = wrap(me + k, owners) * clusters
        aimed = (targets >= low) & (targets < low + clusters)
        first = jnp.min(jnp.where(aimed, position, count - 1))
        last = jnp.max(jnp.where(aimed, position, -1))
        final = jnp.maximum(last, 0)
        chosen_near.append((low, first, final, last >= 0, last > first))
        for i, at in enumerate((first, final)):
            pltpu.make_async_copy(
                near_blocks.at[0, 0, at], picked.at[2 * (k - 1) + i], pick_sems.at[2 * (k - 1) + i]).start()

    waves_in.wait()
    for s in range(clusters):
        real, imag = (waves[c, :, s * PANEL:(s + 1) * PANEL] for c in range(2))
        field[s * rows:s * rows + half, :] = jnp.concatenate([real, -imag], axis=1)
        field[s * rows + half:(s + 1) * rows, :] = jnp.concatenate([imag, real], axis=1)

    dst_in.wait()
    far_in.wait()
    packed = owners * 8 <= 32
    if owners * depth != blocks:
        ordered[...] = jnp.zeros_like(ordered)
        for place in range(owners * depth):
            source_of[place] = 0
    if not packed:
        for k in range(owners):
            counts[k] = 0
    so_far = jnp.int32(0)
    label_row = jnp.zeros((1, LANES), jnp.int32)
    factors_in.wait()
    for f in range(blocks):
        routed = dst_f[0, 0, f]
        owner = div_by(routed, blocks)
        slot = routed - owner * blocks
        ahead = wrap(owner - me, owners)
        if packed:
            shift = ahead * 8
            taken = lax.shift_right_logical(so_far, shift) & 255
            so_far = so_far + lax.shift_left(jnp.int32(1), shift)
        else:
            taken = counts[ahead]
            counts[ahead] = taken + 1
        place = ahead * depth + taken
        at = pl.ds(pl.multiple_of(place * rank, rank), rank)
        ordered[at, 0:PANEL] = factors[0, 0, f, 0]
        ordered[at, PANEL:2 * PANEL] = factors[0, 0, f, 1]
        source_of[place] = src_f[0, 0, f]
        label_row = jnp.where(lane == place, slot + 1, label_row)
    far_labels = jnp.broadcast_to(label_row, (8, LANES)).astype(jnp.float32)
    labels[...] = far_labels

    group = lane // rank
    everything = field[...]
    for k in range(owners):
        out = own_coeffs if k == 0 else messages[k - 1]
        product = dot_nt(everything, ordered[k * chunks * LANES:(k + 1) * chunks * LANES, :])
        for chunk in range(chunks):
            source = jnp.zeros((1, LANES), jnp.int32)
            for at in range(per_chunk):
                source = jnp.where(group == at, source_of[k * depth + chunk * per_chunk + at], source)
            part = product[:, chunk * LANES:(chunk + 1) * LANES]
            chosen = part[0:rows]
            for s in range(1, clusters):
                chosen = jnp.where(source == s, part[s * rows:(s + 1) * rows], chosen)
            out[chunk * rows:(chunk + 1) * rows, :] = chosen.astype(jnp.bfloat16)

    tgt_in.wait()
    near_in.wait()
    near_labels = jnp.zeros((1, LANES), jnp.int32)
    for k, (low, first, final, any_, two) in enumerate(chosen_near, 1):
        near_labels = jnp.where(lane == k, jnp.where(any_, tgt_n[0, 0, first] - low + 1, 0), near_labels)
        total = jnp.zeros((rows, PANEL), jnp.float32)
        for i, (at, used) in enumerate(((first, any_), (final, two))):
            pltpu.make_async_copy(
                near_blocks.at[0, 0, at], picked.at[2 * (k - 1) + i], pick_sems.at[2 * (k - 1) + i]).wait()
            source = pl.ds(pl.multiple_of(src_n[0, 0, at] * rows, rows), rows)
            matrix = jnp.concatenate([picked[2 * (k - 1) + i, 0], picked[2 * (k - 1) + i, 1]], axis=1)
            total = total + jnp.where(used, dot_nt(field[source, :], matrix), 0.0)
        messages[k - 1][chunks * rows:(chunks + 1) * rows, :] = total.astype(jnp.bfloat16)
    near_tile = jnp.broadcast_to(near_labels, (8, LANES)).astype(jnp.float32)
    tile = jnp.concatenate([far_labels, near_tile], axis=0).astype(jnp.bfloat16)
    for message in messages:
        message[(chunks + 1) * rows:, :] = tile


def read_labels(depth, used, k, far_tile, near_tile):
    lane = lax.broadcasted_iota(jnp.int32, (8, LANES), 1) - k * depth
    line = lax.broadcasted_iota(jnp.int32, (8, LANES), 0)
    weight = jnp.zeros((8, LANES), jnp.float32)
    for r in range(used):
        weight = jnp.where((lane == r) & (line == r // PACK), float(BASE ** (r % PACK)), weight)
    lines = -(-used // PACK)
    values = far_tile * weight
    if near_tile is not None:
        values = values + jnp.where((lane == k - k * depth) & (line == lines), near_tile, 0.0)
    sums = jnp.sum(values, axis=1, keepdims=True).astype(jnp.int32)
    slots = []
    for r in range(used):
        if r % PACK == 0:
            word = sums[r // PACK, 0]
        slots.append(lax.shift_right_logical(word, jnp.int32((r % PACK) * (BASE.bit_length() - 1))) & (BASE - 1))
    return slots, (sums[lines, 0] if near_tile is not None else None)


def far_operands(depth, chunks, rows, coeffs):
    half = rows // 2
    values = jnp.concatenate([coeffs[c * rows:(c + 1) * rows, :] for c in range(chunks)], axis=1)
    crossed = jnp.concatenate([-values[half:rows], values[0:half]], axis=0)
    return jnp.concatenate([values, crossed], axis=1)


def far_matrix(depth, holder, slots, spread):
    slots = slots + [0] * (depth - len(slots))
    return jnp.concatenate([spread[holder, slot, part] for part in range(2) for slot in slots], axis=0)


def own_kernel(depth, used, near_src, near_tgt, far_tgt, field, labels, own_coeffs, far_u, near_blocks,
               total, spread, sums):
    me = lax.axis_index("src")
    sharers, rows, width = total.shape
    clusters = sums.shape[0] - 1
    share = clusters // sharers
    blocks, rank = far_u.shape[2], far_u.shape[4]
    chunks = depth * rank // LANES
    sums[...] = jnp.zeros_like(sums)
    for b in range(near_blocks.shape[2]):
        target = near_tgt[0, 0, b] - me * clusters
        target = jnp.where((target >= 0) & (target < clusters), target, clusters)
        source = pl.ds(pl.multiple_of(near_src[0, 0, b] * rows, rows), rows)
        matrix = jnp.concatenate([near_blocks[0, 0, b, 0], near_blocks[0, 0, b, 1]], axis=1)
        sums[target] += dot_nt(field[source, :], matrix)
    zero = jnp.zeros((rank, PANEL), jnp.bfloat16)
    for holder in range(sharers):
        for part in range(2):
            spread[holder, 0, part] = jnp.zeros((rank, width), jnp.bfloat16)
    for slot in range(blocks):
        cluster = far_tgt[0, 0, slot]
        for part in range(2):
            factor = far_u[0, 0, slot, part]
            for c in range(clusters):
                to = (c % share) * PANEL
                spread[c // share, slot + 1, part, :, to:to + PANEL] = jnp.where(cluster == c, factor, zero)
    slots, _ = read_labels(depth, used, 0, labels[...], None)
    left = far_operands(depth, chunks, rows, own_coeffs)
    for holder in range(sharers):
        near = jnp.concatenate([sums[holder * share + c] for c in range(share)], axis=1)
        total[holder] = near + dot_nn(left, far_matrix(depth, holder, slots, spread))


def target_kernel(owners, depth, used, steps, total, spread, *rest):
    messages, outs = rest[:owners - 1], rest[owners - 1:]
    sharers, rows, width = total.shape
    share = width // PANEL
    chunks = depth * spread.shape[3] // LANES
    me = lax.axis_index("tgt")
    holders = [wrap(me + step, sharers) for step in steps]
    sums = [total[holder] for holder in holders]
    read = []
    for k, message in enumerate(messages, 1):
        tile = message[(chunks + 1) * rows:, :].astype(jnp.float32)
        read.append(read_labels(depth, used, k, tile[0:8], tile[8:16]))
    for message, (slots, label) in zip(messages, read):
        near = message[chunks * rows:(chunks + 1) * rows, :].astype(jnp.float32)
        left = far_operands(depth, chunks, rows, message)
        for i, holder in enumerate(holders):
            part = [jnp.where(label == holder * share + c + 1, near, 0.0) for c in range(share)]
            sums[i] = sums[i] + jnp.concatenate(part, axis=1)
            sums[i] = sums[i] + dot_nn(left, far_matrix(depth, holder, slots, spread))
    for out, value in zip(outs, sums):
        out[...] = value.astype(out.dtype).reshape(out.shape)


def body(incident, near_blocks, near_src, near_tgt, far_v, far_src, far_dst, far_u, far_tgt):
    owners = lax.axis_size("src")
    sharers = lax.axis_size("tgt")
    half = incident.shape[1]
    rows = 2 * half
    clusters = incident.shape[2] // PANEL
    width = clusters // sharers * PANEL
    blocks, rank = far_v.shape[2], far_v.shape[4]
    used = max(2, blocks // owners)
    per_chunk = LANES // rank
    depth = -(-used // per_chunk) * per_chunk
    chunks = depth // per_chunk
    bf16, f32, i32 = jnp.bfloat16, jnp.float32, jnp.int32
    shape = jax.ShapeDtypeStruct

    field, labels, own_coeffs, *messages = pl.pallas_call(
        functools.partial(send_kernel, owners, depth),
        out_shape=[shape((clusters * rows, 2 * PANEL), bf16), shape((8, LANES), f32), shape((chunks * rows, LANES), bf16)]
        + [shape(((chunks + 1) * rows + LABEL_ROWS, LANES), bf16)] * (owners - 1),
        in_specs=[HBM] * 7,
        out_specs=[VMEM] * (2 + owners),
        scratch_shapes=[
            pltpu.SMEM(far_src.shape, i32), pltpu.SMEM(far_dst.shape, i32),
            pltpu.SMEM(near_src.shape, i32), pltpu.SMEM(near_tgt.shape, i32),
            pltpu.VMEM(near_tgt.shape, i32),
            pltpu.VMEM(incident.shape, bf16),
            pltpu.VMEM(far_v.shape, bf16),
            pltpu.VMEM((2 * (owners - 1),) + near_blocks.shape[3:], bf16),
            pltpu.VMEM((owners * depth * rank, 2 * PANEL), bf16),
            pltpu.SMEM((owners * depth,), i32),
            pltpu.SMEM((owners,), i32),
            pltpu.SemaphoreType.DMA((7,)),
            pltpu.SemaphoreType.DMA((2 * (owners - 1),)),
        ],
        compiler_params=PARAMS,
        name="send",
    )(far_src, far_dst, near_src, near_tgt, incident, far_v, near_blocks)
    arrived = [
        lax.ppermute(message, "src", [(s, (s + k) % owners) for s in range(owners)])
        for k, message in enumerate(messages, 1)
    ]
    near_count = near_blocks.shape[2]
    total, spread = pl.pallas_call(
        functools.partial(own_kernel, depth, used),
        out_shape=[shape((sharers, rows, width), f32), shape((sharers, blocks + 1, 2, rank, width), bf16)],
        in_specs=[SMEM] * 3 + [VMEM] * 5,
        out_specs=[VMEM] * 2,
        scratch_shapes=[pltpu.VMEM((clusters + 1, rows, PANEL), f32)],
        compiler_params=PARAMS,
        cost_estimate=pl.CostEstimate(
            flops=64 * near_count * rows * PANEL * PANEL, bytes_accessed=near_count * 4 * PANEL * PANEL, transcendentals=0),
        name="own",
    )(near_src, near_tgt, far_tgt, field, labels, own_coeffs, far_u, near_blocks)

    def target(steps, dtype, dims, name):
        return pl.pallas_call(
            functools.partial(target_kernel, owners, depth, used, steps),
            out_shape=[shape(dims, dtype)] * len(steps),
            in_specs=[VMEM] * (2 + owners - 1),
            out_specs=[VMEM] * len(steps),
            compiler_params=PARAMS,
            name=name,
        )(total, spread, *arrived)

    received = []
    if sharers > 1:
        others = target(tuple(range(1, sharers)), bf16, (rows, width), "target_others")
        received = [
            lax.ppermute(other, "tgt", [(t, (t + k) % sharers) for t in range(sharers)])
            for k, other in enumerate(others, 1)
        ]
    (result,) = target((0,), f32, (2, half, width), "target_mine")
    for other in received:
        result = result + other.astype(f32).reshape(result.shape)
    return result


def solution(mesh):
    placed = (
        P(None, "dir", ("groups", "src")),
        P(("groups", "src"), "tgt", None, None, None, None),
        P(("groups", "src"), "tgt", None),
        P(("groups", "src"), "tgt", None),
        P(("groups", "src"), "tgt", None, None, None, None),
        P(("groups", "src"), "tgt", None),
        P(("groups", "src"), "tgt", None),
        P(("groups", "src"), "tgt", None, None, None, None),
        P(("groups", "src"), "tgt", None),
    )
    return jax.shard_map(
        body,
        mesh=mesh,
        in_specs=placed,
        out_specs=P(None, "dir", ("groups", "src", "tgt")),
        check_vma=False,
    )
```

```python
import functools

import jax
import jax.numpy as jnp
from jax import lax
from jax.experimental import pallas as pl
from jax.experimental.pallas import tpu as pltpu
from jax.sharding import PartitionSpec as P

PANEL = 128
LANES = 128
LABEL_ROWS = 16
PACK = 4
BASE = 64
LIMIT = 24 << 20
VMEM = pl.BlockSpec(memory_space=pltpu.VMEM)
SMEM = pl.BlockSpec(memory_space=pltpu.SMEM)
HBM = pl.BlockSpec(memory_space=pltpu.HBM)
PARAMS = pltpu.CompilerParams(vmem_limit_bytes=LIMIT)


def div_by(value, size):
    if size & (size - 1) == 0:
        return lax.shift_right_logical(value, jnp.int32(size.bit_length() - 1))
    return lax.div(value, jnp.int32(size))


def wrap(value, size):
    if size & (size - 1) == 0:
        return value & (size - 1)
    return jnp.where(value < 0, value + size, jnp.where(value >= size, value - size, value))


def dot_nt(left, right):
    return lax.dot_general(left, right, (((1,), (1,)), ((), ())), preferred_element_type=jnp.float32)


def dot_nn(left, right):
    return jnp.dot(left, right, preferred_element_type=jnp.float32)


def send_kernel(owners, depth, far_src, far_dst, near_src, near_tgt, incident, far_v, near_blocks,
                field, labels, own_coeffs, *rest):
    messages, rest = rest[:owners - 1], rest[owners - 1:]
    (src_f, dst_f, src_n, tgt_n, tgt_row, waves, factors, picked, ordered, source_of, counts,
     sems, pick_sems) = rest
    me = lax.axis_index("src")
    half = waves.shape[1]
    rows = 2 * half
    clusters = waves.shape[2] // PANEL
    blocks, rank = factors.shape[2], factors.shape[4]
    count = tgt_row.shape[2]
    per_chunk = LANES // rank
    chunks = depth // per_chunk
    lane = lax.broadcasted_iota(jnp.int32, (1, LANES), 1)

    loads = [
        pltpu.make_async_copy(a, b, sems.at[i])
        for i, (a, b) in enumerate((
            (near_tgt, tgt_row), (near_tgt, tgt_n), (near_src, src_n), (far_dst, dst_f), (far_src, src_f),
            (incident, waves), (far_v, factors)))
    ]
    for load in loads:
        load.start()
    row_in, tgt_in, near_in, dst_in, far_in, waves_in, factors_in = loads

    row_in.wait()
    targets = tgt_row[0]
    position = lax.broadcasted_iota(jnp.int32, targets.shape, 1)
    chosen_near = []
    for k in range(1, owners):
        low = wrap(me + k, owners) * clusters
        aimed = (targets >= low) & (targets < low + clusters)
        first = jnp.min(jnp.where(aimed, position, count - 1))
        last = jnp.max(jnp.where(aimed, position, -1))
        final = jnp.maximum(last, 0)
        chosen_near.append((low, first, final, last >= 0, last > first))
        for i, at in enumerate((first, final)):
            pltpu.make_async_copy(
                near_blocks.at[0, 0, at], picked.at[2 * (k - 1) + i], pick_sems.at[2 * (k - 1) + i]).start()

    waves_in.wait()
    for s in range(clusters):
        real, imag = (waves[c, :, s * PANEL:(s + 1) * PANEL] for c in range(2))
        field[s * rows:s * rows + half, :] = jnp.concatenate([real, -imag], axis=1)
        field[s * rows + half:(s + 1) * rows, :] = jnp.concatenate([imag, real], axis=1)

    dst_in.wait()
    far_in.wait()
    packed = owners * 8 <= 32
    if owners * depth != blocks:
        ordered[...] = jnp.zeros_like(ordered)
        for place in range(owners * depth):
            source_of[place] = 0
    if not packed:
        for k in range(owners):
            counts[k] = 0
    so_far = jnp.int32(0)
    label_row = jnp.zeros((1, LANES), jnp.int32)
    factors_in.wait()
    for f in range(blocks):
        routed = dst_f[0, 0, f]
        owner = div_by(routed, blocks)
        slot = routed - owner * blocks
        ahead = wrap(owner - me, owners)
        if packed:
            shift = ahead * 8
            taken = lax.shift_right_logical(so_far, shift) & 255
            so_far = so_far + lax.shift_left(jnp.int32(1), shift)
        else:
            taken = counts[ahead]
            counts[ahead] = taken + 1
        place = ahead * depth + taken
        at = pl.ds(pl.multiple_of(place * rank, rank), rank)
        ordered[at, 0:PANEL] = factors[0, 0, f, 0]
        ordered[at, PANEL:2 * PANEL] = factors[0, 0, f, 1]
        source_of[place] = src_f[0, 0, f]
        label_row = jnp.where(lane == place, slot + 1, label_row)
    far_labels = jnp.broadcast_to(label_row, (8, LANES)).astype(jnp.float32)
    labels[...] = far_labels

    group = lane // rank
    everything = field[...]
    for k in range(owners):
        out = own_coeffs if k == 0 else messages[k - 1]
        product = dot_nt(everything, ordered[k * chunks * LANES:(k + 1) * chunks * LANES, :])
        for chunk in range(chunks):
            source = jnp.zeros((1, LANES), jnp.int32)
            for at in range(per_chunk):
                source = jnp.where(group == at, source_of[k * depth + chunk * per_chunk + at], source)
            part = product[:, chunk * LANES:(chunk + 1) * LANES]
            chosen = part[0:rows]
            for s in range(1, clusters):
                chosen = jnp.where(source == s, part[s * rows:(s + 1) * rows], chosen)
            out[chunk * rows:(chunk + 1) * rows, :] = chosen.astype(jnp.bfloat16)

    tgt_in.wait()
    near_in.wait()
    near_labels = jnp.zeros((1, LANES), jnp.int32)
    for k, (low, first, final, any_, two) in enumerate(chosen_near, 1):
        near_labels = jnp.where(lane == k, jnp.where(any_, tgt_n[0, 0, first] - low + 1, 0), near_labels)
        total = jnp.zeros((rows, PANEL), jnp.float32)
        for i, (at, used) in enumerate(((first, any_), (final, two))):
            pltpu.make_async_copy(
                near_blocks.at[0, 0, at], picked.at[2 * (k - 1) + i], pick_sems.at[2 * (k - 1) + i]).wait()
            source = pl.ds(pl.multiple_of(src_n[0, 0, at] * rows, rows), rows)
            matrix = jnp.concatenate([picked[2 * (k - 1) + i, 0], picked[2 * (k - 1) + i, 1]], axis=1)
            total = total + jnp.where(used, dot_nt(field[source, :], matrix), 0.0)
        messages[k - 1][chunks * rows:(chunks + 1) * rows, :] = total.astype(jnp.bfloat16)
    near_tile = jnp.broadcast_to(near_labels, (8, LANES)).astype(jnp.float32)
    tile = jnp.concatenate([far_labels, near_tile], axis=0).astype(jnp.bfloat16)
    for message in messages:
        message[(chunks + 1) * rows:, :] = tile


def read_labels(depth, used, k, far_tile, near_tile):
    lane = lax.broadcasted_iota(jnp.int32, (8, LANES), 1) - k * depth
    line = lax.broadcasted_iota(jnp.int32, (8, LANES), 0)
    weight = jnp.zeros((8, LANES), jnp.float32)
    for r in range(used):
        weight = jnp.where((lane == r) & (line == r // PACK), float(BASE ** (r % PACK)), weight)
    lines = -(-used // PACK)
    values = far_tile * weight
    if near_tile is not None:
        values = values + jnp.where((lane == k - k * depth) & (line == lines), near_tile, 0.0)
    sums = jnp.sum(values, axis=1, keepdims=True).astype(jnp.int32)
    slots = []
    for r in range(used):
        if r % PACK == 0:
            word = sums[r // PACK, 0]
        slots.append(lax.shift_right_logical(word, jnp.int32((r % PACK) * (BASE.bit_length() - 1))) & (BASE - 1))
    return slots, (sums[lines, 0] if near_tile is not None else None)


def far_operands(depth, chunks, rows, coeffs):
    half = rows // 2
    values = jnp.concatenate([coeffs[c * rows:(c + 1) * rows, :] for c in range(chunks)], axis=1)
    crossed = jnp.concatenate([-values[half:rows], values[0:half]], axis=0)
    return jnp.concatenate([values, crossed], axis=1)


def far_matrix(depth, holder, slots, spread):
    slots = slots + [0] * (depth - len(slots))
    return jnp.concatenate([spread[holder, slot, part] for part in range(2) for slot in slots], axis=0)


def own_kernel(depth, used, near_src, near_tgt, far_tgt, field, labels, own_coeffs, far_u, near_blocks,
               total, spread, sums):
    me = lax.axis_index("src")
    sharers, rows, width = total.shape
    clusters = sums.shape[0] - 1
    share = clusters // sharers
    blocks, rank = far_u.shape[2], far_u.shape[4]
    chunks = depth * rank // LANES
    sums[...] = jnp.zeros_like(sums)
    for b in range(near_blocks.shape[2]):
        target = near_tgt[0, 0, b] - me * clusters
        target = jnp.where((target >= 0) & (target < clusters), target, clusters)
        source = pl.ds(pl.multiple_of(near_src[0, 0, b] * rows, rows), rows)
        matrix = jnp.concatenate([near_blocks[0, 0, b, 0], near_blocks[0, 0, b, 1]], axis=1)
        sums[target] += dot_nt(field[source, :], matrix)
    zero = jnp.zeros((rank, PANEL), jnp.bfloat16)
    for holder in range(sharers):
        for part in range(2):
            spread[holder, 0, part] = jnp.zeros((rank, width), jnp.bfloat16)
    for slot in range(blocks):
        cluster = far_tgt[0, 0, slot]
        for part in range(2):
            factor = far_u[0, 0, slot, part]
            for c in range(clusters):
                to = (c % share) * PANEL
                spread[c // share, slot + 1, part, :, to:to + PANEL] = jnp.where(cluster == c, factor, zero)
    slots, _ = read_labels(depth, used, 0, labels[...], None)
    left = far_operands(depth, chunks, rows, own_coeffs)
    for holder in range(sharers):
        near = jnp.concatenate([sums[holder * share + c] for c in range(share)], axis=1)
        total[holder] = near + dot_nn(left, far_matrix(depth, holder, slots, spread))


def target_kernel(owners, depth, used, steps, total, spread, *rest):
    messages, outs = rest[:owners - 1], rest[owners - 1:]
    sharers, rows, width = total.shape
    share = width // PANEL
    chunks = depth * spread.shape[3] // LANES
    me = lax.axis_index("tgt")
    holders = [wrap(me + step, sharers) for step in steps]
    sums = [total[holder] for holder in holders]
    read = []
    for k, message in enumerate(messages, 1):
        tile = message[(chunks + 1) * rows:, :].astype(jnp.float32)
        read.append(read_labels(depth, used, k, tile[0:8], tile[8:16]))
    for message, (slots, label) in zip(messages, read):
        near = message[chunks * rows:(chunks + 1) * rows, :].astype(jnp.float32)
        left = far_operands(depth, chunks, rows, message)
        for i, holder in enumerate(holders):
            part = [jnp.where(label == holder * share + c + 1, near, 0.0) for c in range(share)]
            sums[i] = sums[i] + jnp.concatenate(part, axis=1)
            sums[i] = sums[i] + dot_nn(left, far_matrix(depth, holder, slots, spread))
    for out, value in zip(outs, sums):
        out[...] = value.astype(out.dtype).reshape(out.shape)


def body(incident, near_blocks, near_src, near_tgt, far_v, far_src, far_dst, far_u, far_tgt):
    owners = lax.axis_size("src")
    sharers = lax.axis_size("tgt")
    half = incident.shape[1]
    rows = 2 * half
    clusters = incident.shape[2] // PANEL
    width = clusters // sharers * PANEL
    blocks, rank = far_v.shape[2], far_v.shape[4]
    used = max(2, blocks // owners)
    per_chunk = LANES // rank
    depth = -(-used // per_chunk) * per_chunk
    chunks = depth // per_chunk
    bf16, f32, i32 = jnp.bfloat16, jnp.float32, jnp.int32
    shape = jax.ShapeDtypeStruct

    field, labels, own_coeffs, *messages = pl.pallas_call(
        functools.partial(send_kernel, owners, depth),
        out_shape=[shape((clusters * rows, 2 * PANEL), bf16), shape((8, LANES), f32), shape((chunks * rows, LANES), bf16)]
        + [shape(((chunks + 1) * rows + LABEL_ROWS, LANES), bf16)] * (owners - 1),
        in_specs=[HBM] * 7,
        out_specs=[VMEM] * (2 + owners),
        scratch_shapes=[
            pltpu.SMEM(far_src.shape, i32), pltpu.SMEM(far_dst.shape, i32),
            pltpu.SMEM(near_src.shape, i32), pltpu.SMEM(near_tgt.shape, i32),
            pltpu.VMEM(near_tgt.shape, i32),
            pltpu.VMEM(incident.shape, bf16),
            pltpu.VMEM(far_v.shape, bf16),
            pltpu.VMEM((2 * (owners - 1),) + near_blocks.shape[3:], bf16),
            pltpu.VMEM((owners * depth * rank, 2 * PANEL), bf16),
            pltpu.SMEM((owners * depth,), i32),
            pltpu.SMEM((owners,), i32),
            pltpu.SemaphoreType.DMA((7,)),
            pltpu.SemaphoreType.DMA((2 * (owners - 1),)),
        ],
        compiler_params=PARAMS,
        name="send",
    )(*(pltpu.with_memory_space_constraint(array, pltpu.HBM)
        for array in (far_src, far_dst, near_src, near_tgt, incident, far_v, near_blocks)))
    arrived = [
        lax.ppermute(message, "src", [(s, (s + k) % owners) for s in range(owners)])
        for k, message in enumerate(messages, 1)
    ]
    near_count = near_blocks.shape[2]
    total, spread = pl.pallas_call(
        functools.partial(own_kernel, depth, used),
        out_shape=[shape((sharers, rows, width), f32), shape((sharers, blocks + 1, 2, rank, width), bf16)],
        in_specs=[SMEM] * 3 + [VMEM] * 5,
        out_specs=[VMEM] * 2,
        scratch_shapes=[pltpu.VMEM((clusters + 1, rows, PANEL), f32)],
        compiler_params=PARAMS,
        cost_estimate=pl.CostEstimate(
            flops=64 * near_count * rows * PANEL * PANEL, bytes_accessed=near_count * 4 * PANEL * PANEL, transcendentals=0),
        name="own",
    )(near_src, near_tgt, far_tgt, field, labels, own_coeffs, far_u, near_blocks)

    def target(steps, dtype, dims, name):
        return pl.pallas_call(
            functools.partial(target_kernel, owners, depth, used, steps),
            out_shape=[shape(dims, dtype)] * len(steps),
            in_specs=[VMEM] * (2 + owners - 1),
            out_specs=[VMEM] * len(steps),
            compiler_params=PARAMS,
            name=name,
        )(total, spread, *arrived)

    received = []
    if sharers > 1:
        others = target(tuple(range(1, sharers)), bf16, (rows, width), "target_others")
        received = [
            lax.ppermute(other, "tgt", [(t, (t + k) % sharers) for t in range(sharers)])
            for k, other in enumerate(others, 1)
        ]
    (result,) = target((0,), f32, (2, half, width), "target_mine")
    for other in received:
        result = result + other.astype(f32).reshape(result.shape)
    return result


def solution(mesh):
    placed = (
        P(None, "dir", ("groups", "src")),
        P(("groups", "src"), "tgt", None, None, None, None),
        P(("groups", "src"), "tgt", None),
        P(("groups", "src"), "tgt", None),
        P(("groups", "src"), "tgt", None, None, None, None),
        P(("groups", "src"), "tgt", None),
        P(("groups", "src"), "tgt", None),
        P(("groups", "src"), "tgt", None, None, None, None),
        P(("groups", "src"), "tgt", None),
    )
    return jax.shard_map(
        body,
        mesh=mesh,
        in_specs=placed,
        out_specs=P(None, "dir", ("groups", "src", "tgt")),
        check_vma=False,
    )
```

```python
import functools

import jax
import jax.numpy as jnp
from jax import lax
from jax.experimental import pallas as pl
from jax.experimental.pallas import tpu as pltpu
from jax.sharding import PartitionSpec as P

PANEL = 128
LANES = 128
LABEL_ROWS = 16
PACK = 4
BASE = 64
LIMIT = 24 << 20
SEND_LIMIT = 24 << 20
VMEM = pl.BlockSpec(memory_space=pltpu.VMEM)
SMEM = pl.BlockSpec(memory_space=pltpu.SMEM)
HBM = pl.BlockSpec(memory_space=pltpu.HBM)
PARAMS = pltpu.CompilerParams(vmem_limit_bytes=LIMIT)


def in_hbm(array):
    return pltpu.with_memory_space_constraint(array, pltpu.HBM)


def div_by(value, size):
    if size & (size - 1) == 0:
        return lax.shift_right_logical(value, jnp.int32(size.bit_length() - 1))
    return lax.div(value, jnp.int32(size))


def wrap(value, size):
    if size & (size - 1) == 0:
        return value & (size - 1)
    return jnp.where(value < 0, value + size, jnp.where(value >= size, value - size, value))


def dot_nt(left, right):
    return lax.dot_general(left, right, (((1,), (1,)), ((), ())), preferred_element_type=jnp.float32)


def dot_nn(left, right):
    return jnp.dot(left, right, preferred_element_type=jnp.float32)


def send_kernel(owners, depth, far_src, far_dst, near_src, near_tgt, incident, far_v, near_blocks,
                field, labels, own_coeffs, *rest):
    messages, rest = rest[:owners - 1], rest[owners - 1:]
    (src_f, dst_f, src_n, tgt_n, tgt_row, waves, factors, picked, ordered, source_of, counts,
     sems, pick_sems) = rest
    me = lax.axis_index("src")
    half = waves.shape[1]
    rows = 2 * half
    clusters = waves.shape[2] // PANEL
    blocks, rank = factors.shape[2], factors.shape[4]
    count = tgt_row.shape[2]
    per_chunk = LANES // rank
    chunks = depth // per_chunk
    lane = lax.broadcasted_iota(jnp.int32, (1, LANES), 1)

    loads = [
        pltpu.make_async_copy(a, b, sems.at[i])
        for i, (a, b) in enumerate((
            (near_tgt, tgt_row), (near_tgt, tgt_n), (near_src, src_n), (far_dst, dst_f), (far_src, src_f),
            (incident, waves), (far_v, factors)))
    ]
    for load in loads:
        load.start()
    row_in, tgt_in, near_in, dst_in, far_in, waves_in, factors_in = loads

    row_in.wait()
    targets = tgt_row[0]
    position = lax.broadcasted_iota(jnp.int32, targets.shape, 1)
    line = lax.broadcasted_iota(jnp.int32, (-(-2 * (owners - 1) // 8) * 8, 1), 0)
    low_of = wrap(me + 1 + line // 2, owners) * clusters
    aimed = (targets >= low_of) & (targets < low_of + clusters)
    found = jnp.where(aimed, jnp.where(line % 2 == 0, count - 1 - position, position), -1).astype(jnp.float32)
    found = jnp.max(found, axis=1, keepdims=True).astype(jnp.int32)
    chosen_near = []
    for k in range(1, owners):
        low = wrap(me + k, owners) * clusters
        last = found[2 * k - 1, 0]
        final = jnp.maximum(last, 0)
        first = jnp.minimum(count - 1 - found[2 * k - 2, 0], count - 1)
        chosen_near.append((low, first, final, last >= 0, last > first))
    for k, (_, first, final, _, _) in enumerate(chosen_near, 1):
        for i, at in enumerate((first, final)):
            pltpu.make_async_copy(
                near_blocks.at[0, 0, at], picked.at[2 * (k - 1) + i], pick_sems.at[2 * (k - 1) + i]).start()

    waves_in.wait()
    for s in range(clusters):
        real, imag = (waves[c, :, s * PANEL:(s + 1) * PANEL] for c in range(2))
        field[s * rows:s * rows + half, :] = jnp.concatenate([real, -imag], axis=1)
        field[s * rows + half:(s + 1) * rows, :] = jnp.concatenate([imag, real], axis=1)

    dst_in.wait()
    far_in.wait()
    packed = owners * 8 <= 32
    if owners * depth != blocks:
        ordered[...] = jnp.zeros_like(ordered)
        for place in range(owners * depth):
            source_of[place] = 0
    if not packed:
        for k in range(owners):
            counts[k] = 0
    so_far = jnp.int32(0)
    label_row = jnp.zeros((1, LANES), jnp.int32)
    factors_in.wait()
    for f in range(blocks):
        routed = dst_f[0, 0, f]
        owner = div_by(routed, blocks)
        slot = routed - owner * blocks
        ahead = wrap(owner - me, owners)
        if packed:
            shift = ahead * 8
            taken = lax.shift_right_logical(so_far, shift) & 255
            so_far = so_far + lax.shift_left(jnp.int32(1), shift)
        else:
            taken = counts[ahead]
            counts[ahead] = taken + 1
        place = ahead * depth + taken
        at = pl.ds(pl.multiple_of(place * rank, rank), rank)
        ordered[at, 0:PANEL] = factors[0, 0, f, 0]
        ordered[at, PANEL:2 * PANEL] = factors[0, 0, f, 1]
        source_of[place] = src_f[0, 0, f]
        label_row = jnp.where(lane == place, slot + 1, label_row)
    far_labels = jnp.broadcast_to(label_row, (8, LANES)).astype(jnp.float32)
    labels[...] = far_labels

    group = lane // rank
    everything = field[...]
    for k in range(owners):
        out = own_coeffs if k == 0 else messages[k - 1]
        product = dot_nt(everything, ordered[k * chunks * LANES:(k + 1) * chunks * LANES, :])
        for chunk in range(chunks):
            source = jnp.zeros((1, LANES), jnp.int32)
            for at in range(per_chunk):
                source = jnp.where(group == at, source_of[k * depth + chunk * per_chunk + at], source)
            part = product[:, chunk * LANES:(chunk + 1) * LANES]
            chosen = part[0:rows]
            for s in range(1, clusters):
                chosen = jnp.where(source == s, part[s * rows:(s + 1) * rows], chosen)
            out[chunk * rows:(chunk + 1) * rows, :] = chosen.astype(jnp.bfloat16)

    tgt_in.wait()
    near_in.wait()
    near_labels = jnp.zeros((1, LANES), jnp.int32)
    for k, (_, first, final, _, _) in enumerate(chosen_near, 1):
        for i, at in enumerate((first, final)):
            pltpu.make_async_copy(
                near_blocks.at[0, 0, at], picked.at[2 * (k - 1) + i], pick_sems.at[2 * (k - 1) + i]).wait()
    for k, (low, first, final, any_, two) in enumerate(chosen_near, 1):
        near_labels = jnp.where(lane == k, jnp.where(any_, tgt_n[0, 0, first] - low + 1, 0), near_labels)
        left, right = [], []
        for i, (at, used) in enumerate(((first, any_), (final, two))):
            source = pl.ds(pl.multiple_of(src_n[0, 0, at] * rows, rows), rows)
            values = field[source, :]
            left.append(jnp.where(used, values, jnp.zeros_like(values)))
            right += [picked[2 * (k - 1) + i, c] for c in range(2)]
        total = dot_nt(jnp.concatenate(left, axis=1), jnp.concatenate(right, axis=1))
        messages[k - 1][chunks * rows:(chunks + 1) * rows, :] = total.astype(jnp.bfloat16)
    near_tile = jnp.broadcast_to(near_labels, (8, LANES)).astype(jnp.float32)
    tile = jnp.concatenate([far_labels, near_tile], axis=0).astype(jnp.bfloat16)
    for message in messages:
        message[(chunks + 1) * rows:, :] = tile


def read_labels(depth, used, k, far_tile, near_tile):
    lane = lax.broadcasted_iota(jnp.int32, (8, LANES), 1) - k * depth
    line = lax.broadcasted_iota(jnp.int32, (8, LANES), 0)
    weight = jnp.zeros((8, LANES), jnp.float32)
    for r in range(used):
        weight = jnp.where((lane == r) & (line == r // PACK), float(BASE ** (r % PACK)), weight)
    lines = -(-used // PACK)
    values = far_tile * weight
    if near_tile is not None:
        values = values + jnp.where((lane == k - k * depth) & (line == lines), near_tile, 0.0)
    sums = jnp.sum(values, axis=1, keepdims=True).astype(jnp.int32)
    slots = []
    for r in range(used):
        if r % PACK == 0:
            word = sums[r // PACK, 0]
        slots.append(lax.shift_right_logical(word, jnp.int32((r % PACK) * (BASE.bit_length() - 1))) & (BASE - 1))
    return slots, (sums[lines, 0] if near_tile is not None else None)


def far_operands(depth, chunks, rows, coeffs):
    half = rows // 2
    values = jnp.concatenate([coeffs[c * rows:(c + 1) * rows, :] for c in range(chunks)], axis=1)
    crossed = jnp.concatenate([-values[half:rows], values[0:half]], axis=0)
    return jnp.concatenate([values, crossed], axis=1)


def far_matrix(depth, holder, slots, spread):
    slots = slots + [0] * (depth - len(slots))
    return jnp.concatenate([spread[holder, slot, part] for part in range(2) for slot in slots], axis=0)


def own_kernel(depth, used, near_src, near_tgt, far_tgt, field, labels, own_coeffs, far_u, near_blocks,
               total, spread, sums):
    count = near_blocks.shape[2]
    me = lax.axis_index("src")
    sharers, rows, width = total.shape
    clusters = sums.shape[0] - 1
    share = clusters // sharers
    blocks, rank = far_u.shape[2], far_u.shape[4]
    chunks = depth * rank // LANES
    zero = jnp.zeros((rank, PANEL), jnp.bfloat16)
    for holder in range(sharers):
        for part in range(2):
            spread[holder, 0, part] = jnp.zeros((rank, width), jnp.bfloat16)
    for slot in range(blocks):
        cluster = far_tgt[0, 0, slot]
        for part in range(2):
            factor = far_u[0, 0, slot, part]
            for c in range(clusters):
                to = (c % share) * PANEL
                spread[c // share, slot + 1, part, :, to:to + PANEL] = jnp.where(cluster == c, factor, zero)
    slots, _ = read_labels(depth, used, 0, labels[...], None)
    left = far_operands(depth, chunks, rows, own_coeffs)
    for holder in range(sharers):
        far = dot_nn(left, far_matrix(depth, holder, slots, spread))
        for c in range(share):
            sums[holder * share + c] = far[:, c * PANEL:(c + 1) * PANEL]
    for b in range(count):
        target = near_tgt[0, 0, b] - me * clusters
        target = jnp.where((target >= 0) & (target < clusters), target, clusters)
        source = pl.ds(pl.multiple_of(near_src[0, 0, b] * rows, rows), rows)
        matrix = jnp.concatenate([near_blocks[0, 0, b, 0], near_blocks[0, 0, b, 1]], axis=1)
        sums[target] += dot_nt(field[source, :], matrix)
    for holder in range(sharers):
        for c in range(share):
            total[holder, :, c * PANEL:(c + 1) * PANEL] = sums[holder * share + c]


def target_kernel(owners, depth, used, steps, total, spread, *rest):
    messages, outs = rest[:owners - 1], rest[owners - 1:]
    sharers, rows, width = total.shape
    share = width // PANEL
    chunks = depth * spread.shape[3] // LANES
    me = lax.axis_index("tgt")
    holders = [wrap(me + step, sharers) for step in steps]
    sums = [total[holder] for holder in holders]
    read = []
    for k, message in enumerate(messages, 1):
        tile = message[(chunks + 1) * rows:, :].astype(jnp.float32)
        read.append(read_labels(depth, used, k, tile[0:8], tile[8:16]))
    for message, (slots, label) in zip(messages, read):
        near = message[chunks * rows:(chunks + 1) * rows, :].astype(jnp.float32)
        left = far_operands(depth, chunks, rows, message)
        for i, holder in enumerate(holders):
            part = [jnp.where(label == holder * share + c + 1, near, 0.0) for c in range(share)]
            sums[i] = sums[i] + jnp.concatenate(part, axis=1)
            sums[i] = sums[i] + dot_nn(left, far_matrix(depth, holder, slots, spread))
    for out, value in zip(outs, sums):
        out[...] = value.astype(out.dtype).reshape(out.shape)


def body(incident, near_blocks, near_src, near_tgt, far_v, far_src, far_dst, far_u, far_tgt):
    owners = lax.axis_size("src")
    sharers = lax.axis_size("tgt")
    half = incident.shape[1]
    rows = 2 * half
    clusters = incident.shape[2] // PANEL
    width = clusters // sharers * PANEL
    blocks, rank = far_v.shape[2], far_v.shape[4]
    used = max(2, blocks // owners)
    per_chunk = LANES // rank
    depth = -(-used // per_chunk) * per_chunk
    chunks = depth // per_chunk
    bf16, f32, i32 = jnp.bfloat16, jnp.float32, jnp.int32
    shape = jax.ShapeDtypeStruct

    field, labels, own_coeffs, *messages = pl.pallas_call(
        functools.partial(send_kernel, owners, depth),
        out_shape=[shape((clusters * rows, 2 * PANEL), bf16), shape((8, LANES), f32), shape((chunks * rows, LANES), bf16)]
        + [shape(((chunks + 1) * rows + LABEL_ROWS, LANES), bf16)] * (owners - 1),
        in_specs=[HBM] * 7,
        out_specs=[VMEM] * (2 + owners),
        scratch_shapes=[
            pltpu.SMEM(far_src.shape, i32), pltpu.SMEM(far_dst.shape, i32),
            pltpu.SMEM(near_src.shape, i32), pltpu.SMEM(near_tgt.shape, i32),
            pltpu.VMEM(near_tgt.shape, i32),
            pltpu.VMEM(incident.shape, bf16),
            pltpu.VMEM(far_v.shape, bf16),
            pltpu.VMEM((2 * (owners - 1),) + near_blocks.shape[3:], bf16),
            pltpu.VMEM((owners * depth * rank, 2 * PANEL), bf16),
            pltpu.SMEM((owners * depth,), i32),
            pltpu.SMEM((owners,), i32),
            pltpu.SemaphoreType.DMA((7,)),
            pltpu.SemaphoreType.DMA((2 * (owners - 1),)),
        ],
        compiler_params=pltpu.CompilerParams(vmem_limit_bytes=SEND_LIMIT),
        name="send",
    )(*map(in_hbm, (far_src, far_dst, near_src, near_tgt, incident, far_v, near_blocks)))
    arrived = [
        lax.ppermute(message, "src", [(s, (s + k) % owners) for s in range(owners)])
        for k, message in enumerate(messages, 1)
    ]
    near_count = near_blocks.shape[2]
    total, spread = pl.pallas_call(
        functools.partial(own_kernel, depth, used),
        out_shape=[shape((sharers, rows, width), f32), shape((sharers, blocks + 1, 2, rank, width), bf16)],
        in_specs=[SMEM] * 3 + [VMEM] * 5,
        out_specs=[VMEM] * 2,
        scratch_shapes=[pltpu.VMEM((clusters + 1, rows, PANEL), f32)],
        compiler_params=PARAMS,
        cost_estimate=pl.CostEstimate(
            flops=64 * near_count * rows * PANEL * PANEL, bytes_accessed=near_count * 4 * PANEL * PANEL, transcendentals=0),
        name="own",
    )(near_src, near_tgt, far_tgt, field, labels, own_coeffs, far_u, near_blocks)

    def target(steps, dtype, dims, name):
        return pl.pallas_call(
            functools.partial(target_kernel, owners, depth, used, steps),
            out_shape=[shape(dims, dtype)] * len(steps),
            in_specs=[VMEM] * (2 + owners - 1),
            out_specs=[VMEM] * len(steps),
            compiler_params=PARAMS,
            name=name,
        )(total, spread, *arrived)

    received = []
    if sharers > 1:
        others = target(tuple(range(1, sharers)), bf16, (rows, width), "target_others")
        received = [
            lax.ppermute(other, "tgt", [(t, (t + k) % sharers) for t in range(sharers)])
            for k, other in enumerate(others, 1)
        ]
    (result,) = target((0,), f32, (2, half, width), "target_mine")
    for other in received:
        result = result + other.astype(f32).reshape(result.shape)
    return result


def solution(mesh):
    placed = (
        P(None, "dir", ("groups", "src")),
        P(("groups", "src"), "tgt", None, None, None, None),
        P(("groups", "src"), "tgt", None),
        P(("groups", "src"), "tgt", None),
        P(("groups", "src"), "tgt", None, None, None, None),
        P(("groups", "src"), "tgt", None),
        P(("groups", "src"), "tgt", None),
        P(("groups", "src"), "tgt", None, None, None, None),
        P(("groups", "src"), "tgt", None),
    )
    return jax.shard_map(
        body,
        mesh=mesh,
        in_specs=placed,
        out_specs=P(None, "dir", ("groups", "src", "tgt")),
        check_vma=False,
    )
```

```python
import functools

import jax
import jax.numpy as jnp
from jax import lax
from jax.experimental import pallas as pl
from jax.experimental.pallas import tpu as pltpu
from jax.sharding import PartitionSpec as P

PANEL = 128
LANES = 128
LABEL_ROWS = 16
PACK = 4
BASE = 64
LIMIT = 24 << 20
MESSAGE_FLOPS = 2 * 10**9
VMEM = pl.BlockSpec(memory_space=pltpu.VMEM)
SMEM = pl.BlockSpec(memory_space=pltpu.SMEM)
HBM = pl.BlockSpec(memory_space=pltpu.HBM)
PARAMS = pltpu.CompilerParams(vmem_limit_bytes=LIMIT)


def in_hbm(array):
    return pltpu.with_memory_space_constraint(array, pltpu.HBM)


def div_by(value, size):
    if size & (size - 1) == 0:
        return lax.shift_right_logical(value, jnp.int32(size.bit_length() - 1))
    return lax.div(value, jnp.int32(size))


def wrap(value, size):
    if size & (size - 1) == 0:
        return value & (size - 1)
    return jnp.where(value < 0, value + size, jnp.where(value >= size, value - size, value))


def dot_nt(left, right):
    return lax.dot_general(left, right, (((1,), (1,)), ((), ())), preferred_element_type=jnp.float32)


def dot_nn(left, right):
    return jnp.dot(left, right, preferred_element_type=jnp.float32)


def coeff_kernel(owners, depth, far_src, far_dst, near_src, near_tgt, incident, far_v, near_blocks,
                 field, labels, aimed_out, picked, *rest):
    coeffs, rest = rest[:owners], rest[owners:]
    src_f, dst_f, tgt_row, src_row, waves, factors, ordered, source_of, counts, sems, pick_sems = rest
    me = lax.axis_index("src")
    half = waves.shape[1]
    rows = 2 * half
    clusters = waves.shape[2] // PANEL
    blocks, rank = factors.shape[2], factors.shape[4]
    count = tgt_row.shape[2]
    per_chunk = LANES // rank
    chunks = depth // per_chunk
    lane = lax.broadcasted_iota(jnp.int32, (1, LANES), 1)

    loads = [
        pltpu.make_async_copy(a, b, sems.at[i])
        for i, (a, b) in enumerate((
            (near_tgt, tgt_row), (near_src, src_row), (far_dst, dst_f), (far_src, src_f), (incident, waves), (far_v, factors)))
    ]
    for load in loads:
        load.start()
    tgt_in, near_in, dst_in, far_in, waves_in, factors_in = loads

    tgt_in.wait()
    near_in.wait()
    targets = tgt_row[0]
    position = lax.broadcasted_iota(jnp.int32, targets.shape, 1)
    line = lax.broadcasted_iota(jnp.int32, (aimed_out.shape[0], 1), 0)
    low = wrap(me + 1 + line // 2, owners) * clusters
    aimed = (targets >= low) & (targets < low + clusters)
    found = jnp.where(line % 2 == 0, count - 1 - position, position)
    found = (found * clusters + src_row[0]) * clusters + targets - low
    found = jnp.max(jnp.where(aimed, found, -1).astype(jnp.float32), axis=1, keepdims=True)
    aimed_out[...] = jnp.broadcast_to(found.astype(jnp.int32), aimed_out.shape)

    picks = []
    for at in range(2 * (owners - 1)):
        where = div_by(jnp.maximum(found[at, 0].astype(jnp.int32), 0), clusters * clusters)
        if at % 2 == 0:
            where = count - 1 - where
        picks.append(pltpu.make_async_copy(near_blocks.at[0, 0, where], picked.at[at], pick_sems.at[at]))
        picks[-1].start()

    waves_in.wait()
    for s in range(clusters):
        real, imag = (waves[c, :, s * PANEL:(s + 1) * PANEL] for c in range(2))
        field[s * rows:s * rows + half, :] = jnp.concatenate([real, -imag], axis=1)
        field[s * rows + half:(s + 1) * rows, :] = jnp.concatenate([imag, real], axis=1)

    dst_in.wait()
    far_in.wait()
    packed = owners * 8 <= 32
    if owners * depth != blocks:
        ordered[...] = jnp.zeros_like(ordered)
        for place in range(owners * depth):
            source_of[place] = 0
    if not packed:
        for k in range(owners):
            counts[k] = 0
    so_far = jnp.int32(0)
    label_row = jnp.zeros((1, LANES), jnp.int32)
    factors_in.wait()
    for f in range(blocks):
        routed = dst_f[0, 0, f]
        owner = div_by(routed, blocks)
        slot = routed - owner * blocks
        ahead = wrap(owner - me, owners)
        if packed:
            shift = ahead * 8
            taken = lax.shift_right_logical(so_far, shift) & 255
            so_far = so_far + lax.shift_left(jnp.int32(1), shift)
        else:
            taken = counts[ahead]
            counts[ahead] = taken + 1
        place = ahead * depth + taken
        at = pl.ds(pl.multiple_of(place * rank, rank), rank)
        ordered[at, 0:PANEL] = factors[0, 0, f, 0]
        ordered[at, PANEL:2 * PANEL] = factors[0, 0, f, 1]
        source_of[place] = src_f[0, 0, f]
        label_row = jnp.where(lane == place, slot + 1, label_row)
    labels[...] = jnp.broadcast_to(label_row, (8, LANES)).astype(jnp.float32)

    group = lane // rank
    everything = field[...]
    for k in range(owners):
        product = dot_nt(everything, ordered[k * chunks * LANES:(k + 1) * chunks * LANES, :])
        for chunk in range(chunks):
            source = jnp.zeros((1, LANES), jnp.int32)
            for at in range(per_chunk):
                source = jnp.where(group == at, source_of[k * depth + chunk * per_chunk + at], source)
            part = product[:, chunk * LANES:(chunk + 1) * LANES]
            chosen = part[0:rows]
            for s in range(1, clusters):
                chosen = jnp.where(source == s, part[s * rows:(s + 1) * rows], chosen)
            coeffs[k][chunk * rows:(chunk + 1) * rows, :] = chosen.astype(jnp.bfloat16)
    for pick in picks:
        pick.wait()


def message_kernel(owners, count, field, labels, aimed, picked, *rest):
    coeffs, messages = rest[:owners - 1], rest[owners - 1:]
    depth_rows = coeffs[0].shape[0]
    rows = messages[0].shape[0] - depth_rows - LABEL_ROWS
    clusters = field.shape[0] // rows
    lane = lax.broadcasted_iota(jnp.int32, (1, LANES), 1)
    near_labels = jnp.zeros((1, LANES), jnp.int32)
    every = aimed[...]
    for k, (message, part) in enumerate(zip(messages, coeffs), 1):
        first, last = every[2 * k - 2, 0], every[2 * k - 1, 0]
        filled = first >= 0
        positions, left, right = [], [], []
        for number in (jnp.maximum(first, 0), jnp.maximum(last, 0)):
            above = div_by(number, clusters)
            positions.append(div_by(above, clusters))
            source = above - positions[-1] * clusters
            left.append(field[pl.ds(pl.multiple_of(source * rows, rows), rows), :])
            target = number - above * clusters
        positions[0] = count - 1 - positions[0]
        near_labels = jnp.where(lane == k, jnp.where(filled, target + 1, 0), near_labels)
        for i, used in enumerate((filled, positions[1] > positions[0])):
            left[i] = jnp.where(used & filled, left[i], jnp.zeros_like(left[i]))
            right += [picked[2 * (k - 1) + i, c] for c in range(2)]
        total = dot_nt(jnp.concatenate(left, axis=1), jnp.concatenate(right, axis=1))
        message[0:depth_rows, :] = part[...]
        message[depth_rows:depth_rows + rows, :] = total.astype(jnp.bfloat16)
    near_tile = jnp.broadcast_to(near_labels, (8, LANES)).astype(jnp.float32)
    tile = jnp.concatenate([labels[...], near_tile], axis=0).astype(jnp.bfloat16)
    for message in messages:
        message[depth_rows + rows:, :] = tile


def read_labels(depth, used, k, far_tile, near_tile):
    lane = lax.broadcasted_iota(jnp.int32, (8, LANES), 1) - k * depth
    line = lax.broadcasted_iota(jnp.int32, (8, LANES), 0)
    weight = jnp.zeros((8, LANES), jnp.float32)
    for r in range(used):
        weight = jnp.where((lane == r) & (line == r // PACK), float(BASE ** (r % PACK)), weight)
    lines = -(-used // PACK)
    values = far_tile * weight
    if near_tile is not None:
        values = values + jnp.where((lane == k - k * depth) & (line == lines), near_tile, 0.0)
    sums = jnp.sum(values, axis=1, keepdims=True).astype(jnp.int32)
    slots = []
    for r in range(used):
        if r % PACK == 0:
            word = sums[r // PACK, 0]
        slots.append(lax.shift_right_logical(word, jnp.int32((r % PACK) * (BASE.bit_length() - 1))) & (BASE - 1))
    return slots, (sums[lines, 0] if near_tile is not None else None)


def far_operands(depth, chunks, rows, coeffs):
    half = rows // 2
    values = jnp.concatenate([coeffs[c * rows:(c + 1) * rows, :] for c in range(chunks)], axis=1)
    crossed = jnp.concatenate([-values[half:rows], values[0:half]], axis=0)
    return jnp.concatenate([values, crossed], axis=1)


def far_matrix(depth, holder, slots, spread):
    slots = slots + [0] * (depth - len(slots))
    return jnp.concatenate([spread[holder, slot, part] for part in range(2) for slot in slots], axis=0)


def own_kernel(depth, used, near_src, near_tgt, far_tgt, field, labels, own_coeffs, far_u, near_blocks,
               total, spread, sums):
    count = near_blocks.shape[2]
    me = lax.axis_index("src")
    sharers, rows, width = total.shape
    clusters = sums.shape[0] - 1
    share = clusters // sharers
    blocks, rank = far_u.shape[2], far_u.shape[4]
    chunks = depth * rank // LANES
    zero = jnp.zeros((rank, PANEL), jnp.bfloat16)
    for holder in range(sharers):
        for part in range(2):
            spread[holder, 0, part] = jnp.zeros((rank, width), jnp.bfloat16)
    for slot in range(blocks):
        cluster = far_tgt[0, 0, slot]
        for part in range(2):
            factor = far_u[0, 0, slot, part]
            for c in range(clusters):
                to = (c % share) * PANEL
                spread[c // share, slot + 1, part, :, to:to + PANEL] = jnp.where(cluster == c, factor, zero)
    slots, _ = read_labels(depth, used, 0, labels[...], None)
    left = far_operands(depth, chunks, rows, own_coeffs)
    for holder in range(sharers):
        far = dot_nn(left, far_matrix(depth, holder, slots, spread))
        for c in range(share):
            sums[holder * share + c] = far[:, c * PANEL:(c + 1) * PANEL]
    for b in range(count):
        target = near_tgt[0, 0, b] - me * clusters
        target = jnp.where((target >= 0) & (target < clusters), target, clusters)
        source = pl.ds(pl.multiple_of(near_src[0, 0, b] * rows, rows), rows)
        matrix = jnp.concatenate([near_blocks[0, 0, b, 0], near_blocks[0, 0, b, 1]], axis=1)
        sums[target] += dot_nt(field[source, :], matrix)
    for holder in range(sharers):
        for c in range(share):
            total[holder, :, c * PANEL:(c + 1) * PANEL] = sums[holder * share + c]


def target_kernel(owners, depth, used, steps, total, spread, *rest):
    messages, outs = rest[:owners - 1], rest[owners - 1:]
    sharers, rows, width = total.shape
    share = width // PANEL
    chunks = depth * spread.shape[3] // LANES
    me = lax.axis_index("tgt")
    holders = [wrap(me + step, sharers) for step in steps]
    sums = [total[holder] for holder in holders]
    read = []
    for k, message in enumerate(messages, 1):
        tile = message[(chunks + 1) * rows:, :].astype(jnp.float32)
        read.append(read_labels(depth, used, k, tile[0:8], tile[8:16]))
    for message, (slots, label) in zip(messages, read):
        near = message[chunks * rows:(chunks + 1) * rows, :].astype(jnp.float32)
        left = far_operands(depth, chunks, rows, message)
        for i, holder in enumerate(holders):
            part = [jnp.where(label == holder * share + c + 1, near, 0.0) for c in range(share)]
            sums[i] = sums[i] + jnp.concatenate(part, axis=1)
            sums[i] = sums[i] + dot_nn(left, far_matrix(depth, holder, slots, spread))
    for out, value in zip(outs, sums):
        out[...] = value.astype(out.dtype).reshape(out.shape)


def body(incident, near_blocks, near_src, near_tgt, far_v, far_src, far_dst, far_u, far_tgt):
    owners = lax.axis_size("src")
    sharers = lax.axis_size("tgt")
    half = incident.shape[1]
    rows = 2 * half
    clusters = incident.shape[2] // PANEL
    width = clusters // sharers * PANEL
    blocks, rank = far_v.shape[2], far_v.shape[4]
    used = max(2, blocks // owners)
    per_chunk = LANES // rank
    depth = -(-used // per_chunk) * per_chunk
    chunks = depth // per_chunk
    bf16, f32, i32 = jnp.bfloat16, jnp.float32, jnp.int32
    shape = jax.ShapeDtypeStruct

    lines = -(-2 * (owners - 1) // 8) * 8
    near_count = near_blocks.shape[2]
    field, labels, aimed, picked, own_coeffs, *coeffs = pl.pallas_call(
        functools.partial(coeff_kernel, owners, depth),
        out_shape=[shape((clusters * rows, 2 * PANEL), bf16), shape((8, LANES), f32), shape((lines, LANES), i32)]
        + [shape((2 * (owners - 1),) + near_blocks.shape[3:], bf16)]
        + [shape((chunks * rows, LANES), bf16)] * owners,
        in_specs=[HBM] * 7,
        out_specs=[VMEM] * (4 + owners),
        scratch_shapes=[
            pltpu.SMEM(far_src.shape, i32), pltpu.SMEM(far_dst.shape, i32),
            pltpu.VMEM(near_tgt.shape, i32), pltpu.VMEM(near_src.shape, i32),
            pltpu.VMEM(incident.shape, bf16),
            pltpu.VMEM(far_v.shape, bf16),
            pltpu.VMEM((owners * depth * rank, 2 * PANEL), bf16),
            pltpu.SMEM((owners * depth,), i32),
            pltpu.SMEM((owners,), i32),
            pltpu.SemaphoreType.DMA((6,)),
            pltpu.SemaphoreType.DMA((2 * (owners - 1),)),
        ],
        compiler_params=PARAMS,
        name="coefficients",
    )(*map(in_hbm, (far_src, far_dst, near_src, near_tgt, incident, far_v, near_blocks)))
    messages = pl.pallas_call(
        functools.partial(message_kernel, owners, near_count),
        out_shape=[shape(((chunks + 1) * rows + LABEL_ROWS, LANES), bf16)] * (owners - 1),
        in_specs=[VMEM] * (3 + owners),
        out_specs=[VMEM] * (owners - 1),
        compiler_params=PARAMS,
        cost_estimate=pl.CostEstimate(flops=MESSAGE_FLOPS, bytes_accessed=0, transcendentals=0),
        name="messages",
    )(field, labels, aimed, picked, *coeffs)
    arrived = [
        lax.ppermute(message, "src", [(s, (s + k) % owners) for s in range(owners)])
        for k, message in enumerate(messages, 1)
    ]
    total, spread = pl.pallas_call(
        functools.partial(own_kernel, depth, used),
        out_shape=[shape((sharers, rows, width), f32), shape((sharers, blocks + 1, 2, rank, width), bf16)],
        in_specs=[SMEM] * 3 + [VMEM] * 5,
        out_specs=[VMEM] * 2,
        scratch_shapes=[pltpu.VMEM((clusters + 1, rows, PANEL), f32)],
        compiler_params=PARAMS,
        cost_estimate=pl.CostEstimate(
            flops=64 * near_count * rows * PANEL * PANEL, bytes_accessed=near_count * 4 * PANEL * PANEL, transcendentals=0),
        name="own",
    )(near_src, near_tgt, far_tgt, field, labels, own_coeffs, far_u, near_blocks)

    def target(steps, dtype, dims, name):
        return pl.pallas_call(
            functools.partial(target_kernel, owners, depth, used, steps),
            out_shape=[shape(dims, dtype)] * len(steps),
            in_specs=[VMEM] * (2 + owners - 1),
            out_specs=[VMEM] * len(steps),
            compiler_params=PARAMS,
            name=name,
        )(total, spread, *arrived)

    received = []
    if sharers > 1:
        others = target(tuple(range(1, sharers)), bf16, (rows, width), "target_others")
        received = [
            lax.ppermute(other, "tgt", [(t, (t + k) % sharers) for t in range(sharers)])
            for k, other in enumerate(others, 1)
        ]
    (result,) = target((0,), f32, (2, half, width), "target_mine")
    for other in received:
        result = result + other.astype(f32).reshape(result.shape)
    return result


def solution(mesh):
    placed = (
        P(None, "dir", ("groups", "src")),
        P(("groups", "src"), "tgt", None, None, None, None),
        P(("groups", "src"), "tgt", None),
        P(("groups", "src"), "tgt", None),
        P(("groups", "src"), "tgt", None, None, None, None),
        P(("groups", "src"), "tgt", None),
        P(("groups", "src"), "tgt", None),
        P(("groups", "src"), "tgt", None, None, None, None),
        P(("groups", "src"), "tgt", None),
    )
    return jax.shard_map(
        body,
        mesh=mesh,
        in_specs=placed,
        out_specs=P(None, "dir", ("groups", "src", "tgt")),
        check_vma=False,
    )
```

```python
import functools

import jax
import jax.numpy as jnp
from jax import lax
from jax.experimental import pallas as pl
from jax.experimental.pallas import tpu as pltpu
from jax.sharding import PartitionSpec as P

PANEL = 128
LANES = 128
LABEL_ROWS = 16
PACK = 4
BASE = 64
LIMIT = 24 << 20
HAND_ON_FLOPS = 2 * 10**9
VMEM = pl.BlockSpec(memory_space=pltpu.VMEM)
SMEM = pl.BlockSpec(memory_space=pltpu.SMEM)
HBM = pl.BlockSpec(memory_space=pltpu.HBM)
PARAMS = pltpu.CompilerParams(vmem_limit_bytes=LIMIT)


def in_hbm(array):
    return pltpu.with_memory_space_constraint(array, pltpu.HBM)


def div_by(value, size):
    if size & (size - 1) == 0:
        return lax.shift_right_logical(value, jnp.int32(size.bit_length() - 1))
    return lax.div(value, jnp.int32(size))


def wrap(value, size):
    if size & (size - 1) == 0:
        return value & (size - 1)
    return jnp.where(value < 0, value + size, jnp.where(value >= size, value - size, value))


def dot_nt(left, right):
    return lax.dot_general(left, right, (((1,), (1,)), ((), ())), preferred_element_type=jnp.float32)


def dot_nn(left, right):
    return jnp.dot(left, right, preferred_element_type=jnp.float32)


def send_kernel(owners, depth, far_src, far_dst, near_src, near_tgt, incident, far_v, near_blocks,
                field, labels, own_coeffs, *rest):
    messages, rest = rest[:owners - 1], rest[owners - 1:]
    src_f, dst_f, tgt_row, src_row, waves, factors, picked, ordered, source_of, counts, sems, pick_sem = rest
    coeffs = (own_coeffs,) + messages
    me = lax.axis_index("src")
    half = waves.shape[1]
    rows = 2 * half
    clusters = waves.shape[2] // PANEL
    blocks, rank = factors.shape[2], factors.shape[4]
    count = tgt_row.shape[2]
    per_chunk = LANES // rank
    chunks = depth // per_chunk
    lane = lax.broadcasted_iota(jnp.int32, (1, LANES), 1)

    loads = [
        pltpu.make_async_copy(a, b, sems.at[i])
        for i, (a, b) in enumerate((
            (near_tgt, tgt_row), (near_src, src_row), (far_dst, dst_f), (far_src, src_f), (incident, waves), (far_v, factors)))
    ]
    for load in loads:
        load.start()
    tgt_in, near_in, dst_in, far_in, waves_in, factors_in = loads

    tgt_in.wait()
    near_in.wait()
    targets = tgt_row[0]
    position = lax.broadcasted_iota(jnp.int32, targets.shape, 1)
    line = lax.broadcasted_iota(jnp.int32, (-(-2 * (owners - 1) // 8) * 8, 1), 0)
    low = wrap(me + 1 + line // 2, owners) * clusters
    aimed = (targets >= low) & (targets < low + clusters)
    found = jnp.where(line % 2 == 0, count - 1 - position, position)
    found = (found * clusters + src_row[0]) * clusters + targets - low
    found = jnp.max(jnp.where(aimed, found, -1).astype(jnp.float32), axis=1, keepdims=True)
    found = found.astype(jnp.int32)
    near_from = []
    for at in range(2 * (owners - 1)):
        number = found[at, 0]
        near_from.append((number, div_by(jnp.maximum(number, 0), clusters * clusters)))
        where = near_from[-1][1] if at % 2 else count - 1 - near_from[-1][1]
        pltpu.make_async_copy(near_blocks.at[0, 0, where], picked.at[at], pick_sem).start()

    waves_in.wait()
    for s in range(clusters):
        real, imag = (waves[c, :, s * PANEL:(s + 1) * PANEL] for c in range(2))
        field[s * rows:s * rows + half, :] = jnp.concatenate([real, -imag], axis=1)
        field[s * rows + half:(s + 1) * rows, :] = jnp.concatenate([imag, real], axis=1)

    dst_in.wait()
    far_in.wait()
    packed = owners * 8 <= 32
    if owners * depth != blocks:
        ordered[...] = jnp.zeros_like(ordered)
        for place in range(owners * depth):
            source_of[place] = 0
    if not packed:
        for k in range(owners):
            counts[k] = 0
    so_far = jnp.int32(0)
    label_row = jnp.zeros((1, LANES), jnp.int32)
    factors_in.wait()
    for f in range(blocks):
        routed = dst_f[0, 0, f]
        owner = div_by(routed, blocks)
        slot = routed - owner * blocks
        ahead = wrap(owner - me, owners)
        if packed:
            shift = ahead * 8
            taken = lax.shift_right_logical(so_far, shift) & 255
            so_far = so_far + lax.shift_left(jnp.int32(1), shift)
        else:
            taken = counts[ahead]
            counts[ahead] = taken + 1
        place = ahead * depth + taken
        at = pl.ds(pl.multiple_of(place * rank, rank), rank)
        ordered[at, 0:PANEL] = factors[0, 0, f, 0]
        ordered[at, PANEL:2 * PANEL] = factors[0, 0, f, 1]
        source_of[place] = src_f[0, 0, f]
        label_row = jnp.where(lane == place, slot + 1, label_row)
    labels[...] = jnp.broadcast_to(label_row, (8, LANES)).astype(jnp.float32)

    group = lane // rank
    everything = field[...]
    for k in range(owners):
        product = dot_nt(everything, ordered[k * chunks * LANES:(k + 1) * chunks * LANES, :])
        for chunk in range(chunks):
            source = jnp.zeros((1, LANES), jnp.int32)
            for at in range(per_chunk):
                source = jnp.where(group == at, source_of[k * depth + chunk * per_chunk + at], source)
            part = product[:, chunk * LANES:(chunk + 1) * LANES]
            chosen = part[0:rows]
            for s in range(1, clusters):
                chosen = jnp.where(source == s, part[s * rows:(s + 1) * rows], chosen)
            coeffs[k][chunk * rows:(chunk + 1) * rows, :] = chosen.astype(jnp.bfloat16)
    near_labels = jnp.zeros((1, LANES), jnp.int32)
    lefts = []
    for k in range(1, owners):
        filled = near_from[2 * k - 2][0] >= 0
        two = near_from[2 * k - 1][1] > count - 1 - near_from[2 * k - 2][1]
        left = []
        for at, used in ((2 * k - 2, filled), (2 * k - 1, filled & two)):
            number, above = near_from[at]
            number = jnp.maximum(number, 0) - above * (clusters * clusters)
            source = div_by(number, clusters)
            target = number - source * clusters
            values = field[pl.ds(pl.multiple_of(source * rows, rows), rows), :]
            left.append(jnp.where(used, values, jnp.zeros_like(values)))
        lefts.append(jnp.concatenate(left, axis=1))
        near_labels = jnp.where(lane == k, jnp.where(filled, target + 1, 0), near_labels)
    near_tile = jnp.broadcast_to(near_labels, (8, LANES)).astype(jnp.float32)
    tile = jnp.concatenate([labels[...], near_tile], axis=0).astype(jnp.bfloat16)
    for message in messages:
        message[(chunks + 1) * rows:, :] = tile
    pltpu.make_async_copy(picked, picked, pick_sem).wait()
    for k, message in enumerate(messages):
        right = jnp.concatenate([picked[2 * k + i, c] for i in range(2) for c in range(2)], axis=1)
        message[chunks * rows:(chunks + 1) * rows, :] = dot_nt(lefts[k], right).astype(jnp.bfloat16)


def hand_on_kernel(*refs):
    for a, b in zip(refs[:len(refs) // 2], refs[len(refs) // 2:]):
        b[...] = a[...]


def read_labels(depth, used, k, far_tile, near_tile):
    lane = lax.broadcasted_iota(jnp.int32, (8, LANES), 1) - k * depth
    line = lax.broadcasted_iota(jnp.int32, (8, LANES), 0)
    weight = jnp.zeros((8, LANES), jnp.float32)
    for r in range(used):
        weight = jnp.where((lane == r) & (line == r // PACK), float(BASE ** (r % PACK)), weight)
    lines = -(-used // PACK)
    values = far_tile * weight
    if near_tile is not None:
        values = values + jnp.where((lane == k - k * depth) & (line == lines), near_tile, 0.0)
    sums = jnp.sum(values, axis=1, keepdims=True).astype(jnp.int32)
    slots = []
    for r in range(used):
        if r % PACK == 0:
            word = sums[r // PACK, 0]
        slots.append(lax.shift_right_logical(word, jnp.int32((r % PACK) * (BASE.bit_length() - 1))) & (BASE - 1))
    return slots, (sums[lines, 0] if near_tile is not None else None)


def far_operands(depth, chunks, rows, coeffs):
    half = rows // 2
    values = jnp.concatenate([coeffs[c * rows:(c + 1) * rows, :] for c in range(chunks)], axis=1)
    crossed = jnp.concatenate([-values[half:rows], values[0:half]], axis=0)
    return jnp.concatenate([values, crossed], axis=1)


def far_matrix(depth, holder, slots, spread):
    slots = slots + [0] * (depth - len(slots))
    return jnp.concatenate([spread[holder, slot, part] for part in range(2) for slot in slots], axis=0)


def own_kernel(depth, used, near_src, near_tgt, far_tgt, field, labels, own_coeffs, far_u, near_blocks,
               total, spread, sums):
    count = near_blocks.shape[2]
    me = lax.axis_index("src")
    sharers, rows, width = total.shape
    clusters = sums.shape[0] - 1
    share = clusters // sharers
    blocks, rank = far_u.shape[2], far_u.shape[4]
    chunks = depth * rank // LANES
    zero = jnp.zeros((rank, PANEL), jnp.bfloat16)
    for holder in range(sharers):
        for part in range(2):
            spread[holder, 0, part] = jnp.zeros((rank, width), jnp.bfloat16)
    for slot in range(blocks):
        cluster = far_tgt[0, 0, slot]
        for part in range(2):
            factor = far_u[0, 0, slot, part]
            for c in range(clusters):
                to = (c % share) * PANEL
                spread[c // share, slot + 1, part, :, to:to + PANEL] = jnp.where(cluster == c, factor, zero)
    slots, _ = read_labels(depth, used, 0, labels[...], None)
    left = far_operands(depth, chunks, rows, own_coeffs)
    for holder in range(sharers):
        far = dot_nn(left, far_matrix(depth, holder, slots, spread))
        for c in range(share):
            sums[holder * share + c] = far[:, c * PANEL:(c + 1) * PANEL]
    for b in range(count):
        target = near_tgt[0, 0, b] - me * clusters
        target = jnp.where((target >= 0) & (target < clusters), target, clusters)
        source = pl.ds(pl.multiple_of(near_src[0, 0, b] * rows, rows), rows)
        matrix = jnp.concatenate([near_blocks[0, 0, b, 0], near_blocks[0, 0, b, 1]], axis=1)
        sums[target] += dot_nt(field[source, :], matrix)
    for holder in range(sharers):
        for c in range(share):
            total[holder, :, c * PANEL:(c + 1) * PANEL] = sums[holder * share + c]


def add_messages(depth, used, first, messages, holders, sums, spread):
    rows = sums[0].shape[0]
    share = sums[0].shape[1] // PANEL
    chunks = depth * spread.shape[3] // LANES
    read = []
    for k, message in enumerate(messages, first):
        tile = message[(chunks + 1) * rows:, :].astype(jnp.float32)
        read.append(read_labels(depth, used, k, tile[0:8], tile[8:16]))
    for message, (slots, label) in zip(messages, read):
        near = message[chunks * rows:(chunks + 1) * rows, :].astype(jnp.float32)
        left = far_operands(depth, chunks, rows, message)
        for i, holder in enumerate(holders):
            part = [jnp.where(label == holder * share + c + 1, near, 0.0) for c in range(share)]
            sums[i] = sums[i] + jnp.concatenate(part, axis=1)
            sums[i] = sums[i] + dot_nn(left, far_matrix(depth, holder, slots, spread))
    return sums


def first_target_kernel(depth, used, total, spread, *rest):
    messages, out = rest[:-1], rest[-1]
    holders = range(total.shape[0])
    sums = add_messages(depth, used, 1, messages, holders, [total[holder] for holder in holders], spread)
    for holder in holders:
        out[holder] = sums[holder]


def last_target_kernel(depth, used, last, steps, total, spread, message, *outs):
    me = lax.axis_index("tgt")
    holders = [wrap(me + step, total.shape[0]) for step in steps]
    sums = add_messages(depth, used, last, [message], holders, [total[holder] for holder in holders], spread)
    for out, value in zip(outs, sums):
        out[...] = value.astype(out.dtype).reshape(out.shape)


def body(incident, near_blocks, near_src, near_tgt, far_v, far_src, far_dst, far_u, far_tgt):
    owners = lax.axis_size("src")
    sharers = lax.axis_size("tgt")
    half = incident.shape[1]
    rows = 2 * half
    clusters = incident.shape[2] // PANEL
    width = clusters // sharers * PANEL
    blocks, rank = far_v.shape[2], far_v.shape[4]
    used = max(2, blocks // owners)
    per_chunk = LANES // rank
    depth = -(-used // per_chunk) * per_chunk
    chunks = depth // per_chunk
    bf16, f32, i32 = jnp.bfloat16, jnp.float32, jnp.int32
    shape = jax.ShapeDtypeStruct

    near_count = near_blocks.shape[2]
    message_shape = shape(((chunks + 1) * rows + LABEL_ROWS, LANES), bf16)
    field, labels, own_coeffs, *messages = pl.pallas_call(
        functools.partial(send_kernel, owners, depth),
        out_shape=[shape((clusters * rows, 2 * PANEL), bf16), shape((8, LANES), f32), shape((chunks * rows, LANES), bf16)]
        + [message_shape] * (owners - 1),
        in_specs=[HBM] * 7,
        out_specs=[VMEM] * (2 + owners),
        scratch_shapes=[
            pltpu.SMEM(far_src.shape, i32), pltpu.SMEM(far_dst.shape, i32),
            pltpu.VMEM(near_tgt.shape, i32), pltpu.VMEM(near_src.shape, i32),
            pltpu.VMEM(incident.shape, bf16),
            pltpu.VMEM(far_v.shape, bf16),
            pltpu.VMEM((2 * (owners - 1),) + near_blocks.shape[3:], bf16),
            pltpu.VMEM((owners * depth * rank, 2 * PANEL), bf16),
            pltpu.SMEM((owners * depth,), i32),
            pltpu.SMEM((owners,), i32),
            pltpu.SemaphoreType.DMA((6,)),
            pltpu.SemaphoreType.DMA,
        ],
        compiler_params=PARAMS,
        name="send",
    )(*map(in_hbm, (far_src, far_dst, near_src, near_tgt, incident, far_v, near_blocks)))
    messages = pl.pallas_call(
        hand_on_kernel,
        out_shape=[message_shape] * (owners - 1),
        in_specs=[VMEM] * (owners - 1),
        out_specs=[VMEM] * (owners - 1),
        compiler_params=PARAMS,
        cost_estimate=pl.CostEstimate(flops=HAND_ON_FLOPS, bytes_accessed=0, transcendentals=0),
        name="hand_on",
    )(*messages)
    arrived = [
        lax.ppermute(message, "src", [(s, (s + k) % owners) for s in range(owners)])
        for k, message in enumerate(messages, 1)
    ]
    total, spread = pl.pallas_call(
        functools.partial(own_kernel, depth, used),
        out_shape=[shape((sharers, rows, width), f32), shape((sharers, blocks + 1, 2, rank, width), bf16)],
        in_specs=[SMEM] * 3 + [VMEM] * 5,
        out_specs=[VMEM] * 2,
        scratch_shapes=[pltpu.VMEM((clusters + 1, rows, PANEL), f32)],
        compiler_params=PARAMS,
        cost_estimate=pl.CostEstimate(
            flops=64 * near_count * rows * PANEL * PANEL, bytes_accessed=near_count * 4 * PANEL * PANEL, transcendentals=0),
        name="own",
    )(near_src, near_tgt, far_tgt, field, labels, own_coeffs, far_u, near_blocks)

    if owners > 2:
        total = pl.pallas_call(
            functools.partial(first_target_kernel, depth, used),
            out_shape=shape((sharers, rows, width), f32),
            in_specs=[VMEM] * owners,
            out_specs=VMEM,
            compiler_params=PARAMS,
            name="target_first",
        )(total, spread, *arrived[:-1])

    def target(steps, dtype, dims, name):
        return pl.pallas_call(
            functools.partial(last_target_kernel, depth, used, owners - 1, steps),
            out_shape=[shape(dims, dtype)] * len(steps),
            in_specs=[VMEM] * 3,
            out_specs=[VMEM] * len(steps),
            compiler_params=PARAMS,
            name=name,
        )(total, spread, arrived[-1])

    received = []
    if sharers > 1:
        others = target(tuple(range(1, sharers)), bf16, (rows, width), "target_others")
        received = [
            lax.ppermute(other, "tgt", [(t, (t + k) % sharers) for t in range(sharers)])
            for k, other in enumerate(others, 1)
        ]
    (result,) = target((0,), f32, (2, half, width), "target_mine")
    for other in received:
        result = result + other.astype(f32).reshape(result.shape)
    return result


def solution(mesh):
    placed = (
        P(None, "dir", ("groups", "src")),
        P(("groups", "src"), "tgt", None, None, None, None),
        P(("groups", "src"), "tgt", None),
        P(("groups", "src"), "tgt", None),
        P(("groups", "src"), "tgt", None, None, None, None),
        P(("groups", "src"), "tgt", None),
        P(("groups", "src"), "tgt", None),
        P(("groups", "src"), "tgt", None, None, None, None),
        P(("groups", "src"), "tgt", None),
    )
    return jax.shard_map(
        body,
        mesh=mesh,
        in_specs=placed,
        out_specs=P(None, "dir", ("groups", "src", "tgt")),
        check_vma=False,
    )
```

```python
import functools

import jax
import jax.numpy as jnp
from jax import lax
from jax.experimental import pallas as pl
from jax.experimental.pallas import tpu as pltpu
from jax.sharding import PartitionSpec as P

PANEL = 128
LANES = 128
LIMIT = 24 << 20
LATE = 2
HAND_ON_FLOPS = 2 * 10**9
VMEM = pl.BlockSpec(memory_space=pltpu.VMEM)
SMEM = pl.BlockSpec(memory_space=pltpu.SMEM)
HBM = pl.BlockSpec(memory_space=pltpu.HBM)
PARAMS = pltpu.CompilerParams(vmem_limit_bytes=LIMIT)


def in_hbm(array):
    return pltpu.with_memory_space_constraint(array, pltpu.HBM)


def div_by(value, size):
    if size & (size - 1) == 0:
        return lax.shift_right_logical(value, jnp.int32(size.bit_length() - 1))
    return lax.div(value, jnp.int32(size))


def label_count(depth):
    return -(-(depth + 1) // 16) * 16


def wrap(value, size):
    if size & (size - 1) == 0:
        return value & (size - 1)
    return jnp.where(value < 0, value + size, jnp.where(value >= size, value - size, value))


def dot_nt(left, right):
    return lax.dot_general(left, right, (((1,), (1,)), ((), ())), preferred_element_type=jnp.float32)


def dot_nn(left, right):
    return jnp.dot(left, right, preferred_element_type=jnp.float32)


def send_kernel(owners, depth, far_src, far_dst, near_src, near_tgt, incident, far_v, near_blocks,
                field, labels, own_coeffs, *rest):
    messages, rest = rest[:owners - 1], rest[owners - 1:]
    src_f, dst_f, tgt_row, src_row, waves, factors, picked, ordered, source_of, counts, sems, pick_sem = rest
    coeffs = (own_coeffs,) + messages
    me = lax.axis_index("src")
    half = waves.shape[1]
    rows = 2 * half
    clusters = waves.shape[2] // PANEL
    blocks, rank = factors.shape[2], factors.shape[4]
    count = tgt_row.shape[2]
    per_chunk = LANES // rank
    chunks = depth // per_chunk
    lane = lax.broadcasted_iota(jnp.int32, (1, LANES), 1)

    loads = [
        pltpu.make_async_copy(a, b, sems.at[i])
        for i, (a, b) in enumerate((
            (near_tgt, tgt_row), (near_src, src_row), (far_dst, dst_f), (far_src, src_f), (incident, waves), (far_v, factors)))
    ]
    for load in loads:
        load.start()
    tgt_in, near_in, dst_in, far_in, waves_in, factors_in = loads

    tgt_in.wait()
    near_in.wait()
    targets = tgt_row[0]
    position = lax.broadcasted_iota(jnp.int32, targets.shape, 1)
    line = lax.broadcasted_iota(jnp.int32, (-(-2 * (owners - 1) // 8) * 8, 1), 0)
    low = wrap(me + 1 + line // 2, owners) * clusters
    aimed = (targets >= low) & (targets < low + clusters)
    found = jnp.where(line % 2 == 0, count - 1 - position, position)
    found = (found * clusters + src_row[0]) * clusters + targets - low
    found = jnp.max(jnp.where(aimed, found, -1).astype(jnp.float32), axis=1, keepdims=True)
    found = found.astype(jnp.int32)
    near_from = []
    for at in range(2 * (owners - 1)):
        number = found[at, 0]
        near_from.append((number, div_by(jnp.maximum(number, 0), clusters * clusters)))
        where = near_from[-1][1] if at % 2 else count - 1 - near_from[-1][1]
        pltpu.make_async_copy(near_blocks.at[0, 0, where], picked.at[at], pick_sem).start()

    waves_in.wait()
    for s in range(clusters):
        real, imag = (waves[c, :, s * PANEL:(s + 1) * PANEL] for c in range(2))
        field[s * rows:s * rows + half, :] = jnp.concatenate([real, -imag], axis=1)
        field[s * rows + half:(s + 1) * rows, :] = jnp.concatenate([imag, real], axis=1)

    dst_in.wait()
    far_in.wait()
    packed = owners * 8 <= 32
    if owners * depth != blocks:
        ordered[...] = jnp.zeros_like(ordered)
        for place in range(owners * depth):
            source_of[place] = 0
    if not packed:
        for k in range(owners):
            counts[k] = 0
    so_far = jnp.int32(0)
    place_of = lax.broadcasted_iota(jnp.int32, labels.shape, 0)
    label_rows = jnp.zeros(labels.shape, jnp.int32)
    factors_in.wait()
    for f in range(blocks):
        routed = dst_f[0, 0, f]
        owner = div_by(routed, blocks)
        slot = routed - owner * blocks
        ahead = wrap(owner - me, owners)
        if packed:
            shift = ahead * 8
            taken = lax.shift_right_logical(so_far, shift) & 255
            so_far = so_far + lax.shift_left(jnp.int32(1), shift)
        else:
            taken = counts[ahead]
            counts[ahead] = taken + 1
        place = ahead * depth + taken
        at = pl.ds(pl.multiple_of(place * rank, rank), rank)
        ordered[at, 0:PANEL] = factors[0, 0, f, 0]
        ordered[at, PANEL:2 * PANEL] = factors[0, 0, f, 1]
        source_of[place] = src_f[0, 0, f]
        label_rows = jnp.where(place_of == place, slot + 1, label_rows)
    labels[...] = label_rows

    group = lane // rank
    everything = field[...]
    for k in range(owners):
        product = dot_nt(everything, ordered[k * chunks * LANES:(k + 1) * chunks * LANES, :])
        for chunk in range(chunks):
            source = jnp.zeros((1, LANES), jnp.int32)
            for at in range(per_chunk):
                source = jnp.where(group == at, source_of[k * depth + chunk * per_chunk + at], source)
            part = product[:, chunk * LANES:(chunk + 1) * LANES]
            chosen = part[0:rows]
            for s in range(1, clusters):
                chosen = jnp.where(source == s, part[s * rows:(s + 1) * rows], chosen)
            coeffs[k][chunk * rows:(chunk + 1) * rows, :] = chosen.astype(jnp.bfloat16)
    lefts = []
    for k, message in enumerate(messages, 1):
        filled = near_from[2 * k - 2][0] >= 0
        two = near_from[2 * k - 1][1] > count - 1 - near_from[2 * k - 2][1]
        left = []
        for at, used in ((2 * k - 2, filled), (2 * k - 1, filled & two)):
            number, above = near_from[at]
            number = jnp.maximum(number, 0) - above * (clusters * clusters)
            source = div_by(number, clusters)
            target = number - source * clusters
            values = field[pl.ds(pl.multiple_of(source * rows, rows), rows), :]
            left.append(jnp.where(used, values, jnp.zeros_like(values)))
        lefts.append(jnp.concatenate(left, axis=1))
        near_label = jnp.full((label_count(depth) - depth, LANES), jnp.where(filled, target + 1, 0), jnp.int32)
        tile = jnp.concatenate([label_rows[k * depth:(k + 1) * depth], near_label], axis=0)
        message[(chunks + 1) * rows:, :] = tile.astype(jnp.float32).astype(jnp.bfloat16)
    pltpu.make_async_copy(picked, picked, pick_sem).wait()
    for k, message in enumerate(messages):
        right = jnp.concatenate([picked[2 * k + i, c] for i in range(2) for c in range(2)], axis=1)
        message[chunks * rows:(chunks + 1) * rows, :] = dot_nt(lefts[k], right).astype(jnp.bfloat16)


def hand_on_kernel(*refs):
    for a, b in zip(refs[:len(refs) // 2], refs[len(refs) // 2:]):
        b[...] = a[...]


def read_labels(used, tile):
    return [tile[r, 0] for r in range(used)]


def far_operands(depth, chunks, rows, coeffs):
    half = rows // 2
    values = jnp.concatenate([coeffs[c * rows:(c + 1) * rows, :] for c in range(chunks)], axis=1)
    crossed = jnp.concatenate([-values[half:rows], values[0:half]], axis=0)
    return jnp.concatenate([values, crossed], axis=1)


def far_matrix(depth, holder, slots, spread):
    slots = slots + [0] * (depth - len(slots))
    return jnp.concatenate([spread[holder, slot, part] for part in range(2) for slot in slots], axis=0)


def own_kernel(depth, used, near_src, near_tgt, far_tgt, field, labels, own_coeffs, far_u, near_blocks,
               total, spread, sums):
    count = near_blocks.shape[2]
    me = lax.axis_index("src")
    sharers, rows, width = total.shape
    clusters = sums.shape[0] - 1
    share = clusters // sharers
    blocks, rank = far_u.shape[2], far_u.shape[4]
    chunks = depth * rank // LANES
    zero = jnp.zeros((rank, PANEL), jnp.bfloat16)
    for holder in range(sharers):
        for part in range(2):
            spread[holder, 0, part] = jnp.zeros((rank, width), jnp.bfloat16)
    for slot in range(blocks):
        cluster = far_tgt[0, 0, slot]
        for part in range(2):
            factor = far_u[0, 0, slot, part]
            for c in range(clusters):
                to = (c % share) * PANEL
                spread[c // share, slot + 1, part, :, to:to + PANEL] = jnp.where(cluster == c, factor, zero)
    slots = read_labels(used, labels[0:depth, :])
    left = far_operands(depth, chunks, rows, own_coeffs)
    for holder in range(sharers):
        far = dot_nn(left, far_matrix(depth, holder, slots, spread))
        for c in range(share):
            sums[holder * share + c] = far[:, c * PANEL:(c + 1) * PANEL]
    for b in range(count):
        target = near_tgt[0, 0, b] - me * clusters
        target = jnp.where((target >= 0) & (target < clusters), target, clusters)
        source = pl.ds(pl.multiple_of(near_src[0, 0, b] * rows, rows), rows)
        matrix = jnp.concatenate([near_blocks[0, 0, b, 0], near_blocks[0, 0, b, 1]], axis=1)
        sums[target] += dot_nt(field[source, :], matrix)
    for holder in range(sharers):
        for c in range(share):
            total[holder, :, c * PANEL:(c + 1) * PANEL] = sums[holder * share + c]


def add_messages(depth, used, messages, holders, sums, spread):
    rows = sums[0].shape[0]
    share = sums[0].shape[1] // PANEL
    chunks = depth * spread.shape[3] // LANES
    read = []
    for message in messages:
        tile = message[(chunks + 1) * rows:, :].astype(jnp.float32).astype(jnp.int32)
        read.append((read_labels(used, tile), tile[depth, 0]))
    for message, (slots, label) in zip(messages, read):
        near = message[chunks * rows:(chunks + 1) * rows, :].astype(jnp.float32)
        left = far_operands(depth, chunks, rows, message)
        for i, holder in enumerate(holders):
            part = [jnp.where(label == holder * share + c + 1, near, 0.0) for c in range(share)]
            sums[i] = sums[i] + jnp.concatenate(part, axis=1)
            sums[i] = sums[i] + dot_nn(left, far_matrix(depth, holder, slots, spread))
    return sums


def first_target_kernel(depth, used, total, spread, *rest):
    messages, out = rest[:-1], rest[-1]
    holders = range(total.shape[0])
    sums = add_messages(depth, used, messages, holders, [total[holder] for holder in holders], spread)
    for holder in holders:
        out[holder] = sums[holder]


def last_target_kernel(depth, used, late, steps, total, spread, *rest):
    messages, outs = rest[:late], rest[late:]
    me = lax.axis_index("tgt")
    holders = [wrap(me + step, total.shape[0]) for step in steps]
    sums = add_messages(depth, used, messages, holders, [total[holder] for holder in holders], spread)
    for out, value in zip(outs, sums):
        out[...] = value.astype(out.dtype).reshape(out.shape)


def body(incident, near_blocks, near_src, near_tgt, far_v, far_src, far_dst, far_u, far_tgt):
    owners = lax.axis_size("src")
    sharers = lax.axis_size("tgt")
    half = incident.shape[1]
    rows = 2 * half
    clusters = incident.shape[2] // PANEL
    width = clusters // sharers * PANEL
    blocks, rank = far_v.shape[2], far_v.shape[4]
    used = max(2, blocks // owners)
    per_chunk = LANES // rank
    depth = -(-used // per_chunk) * per_chunk
    chunks = depth // per_chunk
    bf16, f32, i32 = jnp.bfloat16, jnp.float32, jnp.int32
    shape = jax.ShapeDtypeStruct

    near_count = near_blocks.shape[2]
    message_shape = shape(((chunks + 1) * rows + label_count(depth), LANES), bf16)
    field, labels, own_coeffs, *messages = pl.pallas_call(
        functools.partial(send_kernel, owners, depth),
        out_shape=[shape((clusters * rows, 2 * PANEL), bf16), shape((owners * depth, LANES), i32), shape((chunks * rows, LANES), bf16)]
        + [message_shape] * (owners - 1),
        in_specs=[HBM] * 7,
        out_specs=[VMEM] * (2 + owners),
        scratch_shapes=[
            pltpu.SMEM(far_src.shape, i32), pltpu.SMEM(far_dst.shape, i32),
            pltpu.VMEM(near_tgt.shape, i32), pltpu.VMEM(near_src.shape, i32),
            pltpu.VMEM(incident.shape, bf16),
            pltpu.VMEM(far_v.shape, bf16),
            pltpu.VMEM((2 * (owners - 1),) + near_blocks.shape[3:], bf16),
            pltpu.VMEM((owners * depth * rank, 2 * PANEL), bf16),
            pltpu.SMEM((owners * depth,), i32),
            pltpu.SMEM((owners,), i32),
            pltpu.SemaphoreType.DMA((6,)),
            pltpu.SemaphoreType.DMA,
        ],
        compiler_params=PARAMS,
        name="send",
    )(*map(in_hbm, (far_src, far_dst, near_src, near_tgt, incident, far_v, near_blocks)))
    messages = pl.pallas_call(
        hand_on_kernel,
        out_shape=[message_shape] * (owners - 1),
        in_specs=[VMEM] * (owners - 1),
        out_specs=[VMEM] * (owners - 1),
        compiler_params=PARAMS,
        cost_estimate=pl.CostEstimate(flops=HAND_ON_FLOPS, bytes_accessed=0, transcendentals=0),
        name="hand_on",
    )(*messages)
    arrived = [
        lax.ppermute(message, "src", [(s, (s + k) % owners) for s in range(owners)])
        for k, message in enumerate(messages, 1)
    ]
    total, spread = pl.pallas_call(
        functools.partial(own_kernel, depth, used),
        out_shape=[shape((sharers, rows, width), f32), shape((sharers, blocks + 1, 2, rank, width), bf16)],
        in_specs=[SMEM] * 3 + [VMEM] * 5,
        out_specs=[VMEM] * 2,
        scratch_shapes=[pltpu.VMEM((clusters + 1, rows, PANEL), f32)],
        compiler_params=PARAMS,
        cost_estimate=pl.CostEstimate(
            flops=64 * near_count * rows * PANEL * PANEL, bytes_accessed=near_count * 4 * PANEL * PANEL, transcendentals=0),
        name="own",
    )(near_src, near_tgt, far_tgt, field, labels, own_coeffs, far_u, near_blocks)

    late = min(LATE, len(arrived))
    if late < len(arrived):
        total = pl.pallas_call(
            functools.partial(first_target_kernel, depth, used),
            out_shape=shape((sharers, rows, width), f32),
            in_specs=[VMEM] * (2 + len(arrived) - late),
            out_specs=VMEM,
            compiler_params=PARAMS,
            name="target_first",
        )(total, spread, *arrived[:len(arrived) - late])

    def target(steps, dtype, dims, name):
        return pl.pallas_call(
            functools.partial(last_target_kernel, depth, used, late, steps),
            out_shape=[shape(dims, dtype)] * len(steps),
            in_specs=[VMEM] * (2 + late),
            out_specs=[VMEM] * len(steps),
            compiler_params=PARAMS,
            name=name,
        )(total, spread, *arrived[len(arrived) - late:])

    received = []
    if sharers > 1:
        others = target(tuple(range(1, sharers)), bf16, (rows, width), "target_others")
        received = [
            lax.ppermute(other, "tgt", [(t, (t + k) % sharers) for t in range(sharers)])
            for k, other in enumerate(others, 1)
        ]
    (result,) = target((0,), f32, (2, half, width), "target_mine")
    for other in received:
        result = result + other.astype(f32).reshape(result.shape)
    return result


def solution(mesh):
    placed = (
        P(None, "dir", ("groups", "src")),
        P(("groups", "src"), "tgt", None, None, None, None),
        P(("groups", "src"), "tgt", None),
        P(("groups", "src"), "tgt", None),
        P(("groups", "src"), "tgt", None, None, None, None),
        P(("groups", "src"), "tgt", None),
        P(("groups", "src"), "tgt", None),
        P(("groups", "src"), "tgt", None, None, None, None),
        P(("groups", "src"), "tgt", None),
    )
    return jax.shard_map(
        body,
        mesh=mesh,
        in_specs=placed,
        out_specs=P(None, "dir", ("groups", "src", "tgt")),
        check_vma=False,
    )
```

```python
import functools

import jax
import jax.numpy as jnp
from jax import lax
from jax.experimental import pallas as pl
from jax.experimental.pallas import tpu as pltpu
from jax.sharding import PartitionSpec as P

PANEL = 128
LANES = 128
LIMIT = 24 << 20
LATE = 1
HAND_ON_FLOPS = 2 * 10**9
VMEM = pl.BlockSpec(memory_space=pltpu.VMEM)
SMEM = pl.BlockSpec(memory_space=pltpu.SMEM)
HBM = pl.BlockSpec(memory_space=pltpu.HBM)
PARAMS = pltpu.CompilerParams(vmem_limit_bytes=LIMIT)


def in_hbm(array):
    return pltpu.with_memory_space_constraint(array, pltpu.HBM)


def div_by(value, size):
    if size & (size - 1) == 0:
        return lax.shift_right_logical(value, jnp.int32(size.bit_length() - 1))
    return lax.div(value, jnp.int32(size))


def label_count(depth):
    return -(-(depth + 1) // 16) * 16


def ring_place(owner, owners):
    if owners != 4:
        return owner
    return (owner & 1) * 2 + (owner >= 2) * 1


def wrap(value, size):
    if size & (size - 1) == 0:
        return value & (size - 1)
    return jnp.where(value < 0, value + size, jnp.where(value >= size, value - size, value))


def dot_nt(left, right):
    return lax.dot_general(left, right, (((1,), (1,)), ((), ())), preferred_element_type=jnp.float32)


def dot_nn(left, right):
    return jnp.dot(left, right, preferred_element_type=jnp.float32)


def send_kernel(owners, depth, far_src, far_dst, near_src, near_tgt, incident, far_v, near_blocks,
                field, labels, own_coeffs, tgt_row, src_row, *rest):
    messages, rest = rest[:owners - 1], rest[owners - 1:]
    src_f, dst_f, waves, factors, picked, ordered, source_of, counts, sems, pick_sem = rest
    coeffs = (own_coeffs,) + messages
    my_place = ring_place(lax.axis_index("src"), owners)
    half = waves.shape[1]
    rows = 2 * half
    clusters = waves.shape[2] // PANEL
    blocks, rank = factors.shape[2], factors.shape[4]
    count = tgt_row.shape[2]
    per_chunk = LANES // rank
    chunks = depth // per_chunk
    lane = lax.broadcasted_iota(jnp.int32, (1, LANES), 1)

    loads = [
        pltpu.make_async_copy(a, b, sems.at[i])
        for i, (a, b) in enumerate((
            (near_tgt, tgt_row), (near_src, src_row), (far_dst, dst_f), (far_src, src_f), (incident, waves), (far_v, factors)))
    ]
    for load in loads:
        load.start()
    tgt_in, near_in, dst_in, far_in, waves_in, factors_in = loads

    tgt_in.wait()
    near_in.wait()
    targets = tgt_row[0]
    position = lax.broadcasted_iota(jnp.int32, targets.shape, 1)
    line = lax.broadcasted_iota(jnp.int32, (-(-2 * (owners - 1) // 8) * 8, 1), 0)
    low = ring_place(wrap(my_place + 1 + line // 2, owners), owners) * clusters
    aimed = (targets >= low) & (targets < low + clusters)
    found = jnp.where(line % 2 == 0, count - 1 - position, position)
    found = (found * clusters + src_row[0]) * clusters + targets - low
    found = jnp.max(jnp.where(aimed, found, -1).astype(jnp.float32), axis=1, keepdims=True)
    found = found.astype(jnp.int32)
    near_from = []
    for at in range(2 * (owners - 1)):
        number = found[at, 0]
        near_from.append((number, div_by(jnp.maximum(number, 0), clusters * clusters)))
        where = near_from[-1][1] if at % 2 else count - 1 - near_from[-1][1]
        pltpu.make_async_copy(near_blocks.at[0, 0, where], picked.at[at], pick_sem).start()

    waves_in.wait()
    for s in range(clusters):
        real, imag = (waves[c, :, s * PANEL:(s + 1) * PANEL] for c in range(2))
        field[s * rows:s * rows + half, :] = jnp.concatenate([real, -imag], axis=1)
        field[s * rows + half:(s + 1) * rows, :] = jnp.concatenate([imag, real], axis=1)

    dst_in.wait()
    far_in.wait()
    packed = owners * 8 <= 32
    if owners * depth != blocks:
        ordered[...] = jnp.zeros_like(ordered)
        for place in range(owners * depth):
            source_of[place] = 0
    if not packed:
        for k in range(owners):
            counts[k] = 0
    so_far = jnp.int32(0)
    place_of = lax.broadcasted_iota(jnp.int32, labels.shape, 0)
    label_rows = jnp.zeros(labels.shape, jnp.int32)
    factors_in.wait()
    for f in range(blocks):
        routed = dst_f[0, 0, f]
        owner = div_by(routed, blocks)
        slot = routed - owner * blocks
        ahead = wrap(ring_place(owner, owners) - my_place, owners)
        if packed:
            shift = ahead * 8
            taken = lax.shift_right_logical(so_far, shift) & 255
            so_far = so_far + lax.shift_left(jnp.int32(1), shift)
        else:
            taken = counts[ahead]
            counts[ahead] = taken + 1
        place = ahead * depth + taken
        at = pl.ds(pl.multiple_of(place * rank, rank), rank)
        ordered[at, 0:PANEL] = factors[0, 0, f, 0]
        ordered[at, PANEL:2 * PANEL] = factors[0, 0, f, 1]
        source_of[place] = src_f[0, 0, f]
        label_rows = jnp.where(place_of == place, slot + 1, label_rows)
    labels[...] = label_rows

    group = lane // rank
    everything = field[...]
    for k in range(owners):
        product = dot_nt(everything, ordered[k * chunks * LANES:(k + 1) * chunks * LANES, :])
        for chunk in range(chunks):
            source = jnp.zeros((1, LANES), jnp.int32)
            for at in range(per_chunk):
                source = jnp.where(group == at, source_of[k * depth + chunk * per_chunk + at], source)
            part = product[:, chunk * LANES:(chunk + 1) * LANES]
            chosen = part[0:rows]
            for s in range(1, clusters):
                chosen = jnp.where(source == s, part[s * rows:(s + 1) * rows], chosen)
            coeffs[k][chunk * rows:(chunk + 1) * rows, :] = chosen.astype(jnp.bfloat16)
    lefts = []
    for k, message in enumerate(messages, 1):
        filled = near_from[2 * k - 2][0] >= 0
        two = near_from[2 * k - 1][1] > count - 1 - near_from[2 * k - 2][1]
        left = []
        for at, used in ((2 * k - 2, filled), (2 * k - 1, filled & two)):
            number, above = near_from[at]
            number = jnp.maximum(number, 0) - above * (clusters * clusters)
            source = div_by(number, clusters)
            target = number - source * clusters
            values = field[pl.ds(pl.multiple_of(source * rows, rows), rows), :]
            left.append(jnp.where(used, values, jnp.zeros_like(values)))
        lefts.append(jnp.concatenate(left, axis=1))
        near_label = jnp.full((label_count(depth) - depth, LANES), jnp.where(filled, target + 1, 0), jnp.int32)
        tile = jnp.concatenate([label_rows[k * depth:(k + 1) * depth], near_label], axis=0)
        message[(chunks + 1) * rows:, :] = tile.astype(jnp.float32).astype(jnp.bfloat16)
    pltpu.make_async_copy(picked, picked, pick_sem).wait()
    for k, message in enumerate(messages):
        right = jnp.concatenate([picked[2 * k + i, c] for i in range(2) for c in range(2)], axis=1)
        message[chunks * rows:(chunks + 1) * rows, :] = dot_nt(lefts[k], right).astype(jnp.bfloat16)


def hand_on_kernel(*refs):
    for a, b in zip(refs[:len(refs) // 2], refs[len(refs) // 2:]):
        b[...] = a[...]


def read_labels(used, tile):
    return [tile[r, 0] for r in range(used)]


def far_operands(depth, chunks, rows, coeffs):
    half = rows // 2
    values = jnp.concatenate([coeffs[c * rows:(c + 1) * rows, :] for c in range(chunks)], axis=1)
    crossed = jnp.concatenate([-values[half:rows], values[0:half]], axis=0)
    return jnp.concatenate([values, crossed], axis=1)


def far_matrix(depth, holder, slots, spread):
    slots = slots + [0] * (depth - len(slots))
    return jnp.concatenate([spread[holder, slot, part] for part in range(2) for slot in slots], axis=0)


def own_kernel(depth, used, near_src, near_tgt, far_tgt, field, labels, own_coeffs, far_u, near_blocks,
               total, spread, sums):
    count = near_blocks.shape[2]
    me = lax.axis_index("src")
    sharers, rows, width = total.shape
    clusters = sums.shape[0] - 1
    share = clusters // sharers
    blocks, rank = far_u.shape[2], far_u.shape[4]
    chunks = depth * rank // LANES
    zero = jnp.zeros((rank, PANEL), jnp.bfloat16)
    for holder in range(sharers):
        for part in range(2):
            spread[holder, 0, part] = jnp.zeros((rank, width), jnp.bfloat16)
    for slot in range(blocks):
        cluster = far_tgt[0, 0, slot]
        for part in range(2):
            factor = far_u[0, 0, slot, part]
            for c in range(clusters):
                to = (c % share) * PANEL
                spread[c // share, slot + 1, part, :, to:to + PANEL] = jnp.where(cluster == c, factor, zero)
    slots = read_labels(used, labels[0:depth, :])
    left = far_operands(depth, chunks, rows, own_coeffs)
    for holder in range(sharers):
        far = dot_nn(left, far_matrix(depth, holder, slots, spread))
        for c in range(share):
            sums[holder * share + c] = far[:, c * PANEL:(c + 1) * PANEL]
    for b in range(count):
        target = near_tgt[0, 0, b] - me * clusters
        target = jnp.where((target >= 0) & (target < clusters), target, clusters)
        source = pl.ds(pl.multiple_of(near_src[0, 0, b] * rows, rows), rows)
        matrix = jnp.concatenate([near_blocks[0, 0, b, 0], near_blocks[0, 0, b, 1]], axis=1)
        sums[target] += dot_nt(field[source, :], matrix)
    for holder in range(sharers):
        for c in range(share):
            total[holder, :, c * PANEL:(c + 1) * PANEL] = sums[holder * share + c]


def add_messages(depth, used, messages, holders, sums, spread):
    rows = sums[0].shape[0]
    share = sums[0].shape[1] // PANEL
    chunks = depth * spread.shape[3] // LANES
    read = []
    for message in messages:
        tile = message[(chunks + 1) * rows:, :].astype(jnp.float32).astype(jnp.int32)
        read.append((read_labels(used, tile), tile[depth, 0]))
    for message, (slots, label) in zip(messages, read):
        near = message[chunks * rows:(chunks + 1) * rows, :].astype(jnp.float32)
        left = far_operands(depth, chunks, rows, message)
        for i, holder in enumerate(holders):
            part = [jnp.where(label == holder * share + c + 1, near, 0.0) for c in range(share)]
            sums[i] = sums[i] + jnp.concatenate(part, axis=1)
            sums[i] = sums[i] + dot_nn(left, far_matrix(depth, holder, slots, spread))
    return sums


def first_target_kernel(depth, used, total, spread, *rest):
    messages, out = rest[:-1], rest[-1]
    holders = range(total.shape[0])
    sums = add_messages(depth, used, messages, holders, [total[holder] for holder in holders], spread)
    for holder in holders:
        out[holder] = sums[holder]


def last_target_kernel(depth, used, late, steps, total, spread, *rest):
    messages, outs = rest[:late], rest[late:]
    me = lax.axis_index("tgt")
    holders = [wrap(me + step, total.shape[0]) for step in steps]
    sums = add_messages(depth, used, messages, holders, [total[holder] for holder in holders], spread)
    for out, value in zip(outs, sums):
        out[...] = value.astype(out.dtype).reshape(out.shape)


def body(incident, near_blocks, near_src, near_tgt, far_v, far_src, far_dst, far_u, far_tgt):
    owners = lax.axis_size("src")
    sharers = lax.axis_size("tgt")
    half = incident.shape[1]
    rows = 2 * half
    clusters = incident.shape[2] // PANEL
    width = clusters // sharers * PANEL
    blocks, rank = far_v.shape[2], far_v.shape[4]
    used = max(2, blocks // owners)
    per_chunk = LANES // rank
    depth = -(-used // per_chunk) * per_chunk
    chunks = depth // per_chunk
    bf16, f32, i32 = jnp.bfloat16, jnp.float32, jnp.int32
    shape = jax.ShapeDtypeStruct

    near_count = near_blocks.shape[2]
    message_shape = shape(((chunks + 1) * rows + label_count(depth), LANES), bf16)
    field, labels, own_coeffs, tgt_row, src_row, *messages = pl.pallas_call(
        functools.partial(send_kernel, owners, depth),
        out_shape=[shape((clusters * rows, 2 * PANEL), bf16), shape((owners * depth, LANES), i32), shape((chunks * rows, LANES), bf16)]
        + [shape(near_tgt.shape, i32), shape(near_src.shape, i32)] + [message_shape] * (owners - 1),
        in_specs=[HBM] * 7,
        out_specs=[VMEM] * (4 + owners),
        scratch_shapes=[
            pltpu.SMEM(far_src.shape, i32), pltpu.SMEM(far_dst.shape, i32),
            pltpu.VMEM(incident.shape, bf16),
            pltpu.VMEM(far_v.shape, bf16),
            pltpu.VMEM((2 * (owners - 1),) + near_blocks.shape[3:], bf16),
            pltpu.VMEM((owners * depth * rank, 2 * PANEL), bf16),
            pltpu.SMEM((owners * depth,), i32),
            pltpu.SMEM((owners,), i32),
            pltpu.SemaphoreType.DMA((6,)),
            pltpu.SemaphoreType.DMA,
        ],
        compiler_params=PARAMS,
        name="send",
    )(*map(in_hbm, (far_src, far_dst, near_src, near_tgt, incident, far_v, near_blocks)))
    messages = pl.pallas_call(
        hand_on_kernel,
        out_shape=[message_shape] * (owners - 1),
        in_specs=[VMEM] * (owners - 1),
        out_specs=[VMEM] * (owners - 1),
        compiler_params=PARAMS,
        cost_estimate=pl.CostEstimate(flops=HAND_ON_FLOPS, bytes_accessed=0, transcendentals=0),
        name="hand_on",
    )(*messages)
    arrived = []
    for k in (1, 3, 2) if owners == 4 else range(1, owners):
        pairs = [(s, ring_place((ring_place(s, owners) + k) % owners, owners)) for s in range(owners)]
        arrived.append(lax.ppermute(messages[k - 1], "src", pairs))
    total, spread = pl.pallas_call(
        functools.partial(own_kernel, depth, used),
        out_shape=[shape((sharers, rows, width), f32), shape((sharers, blocks + 1, 2, rank, width), bf16)],
        in_specs=[SMEM] * 3 + [VMEM] * 5,
        out_specs=[VMEM] * 2,
        scratch_shapes=[pltpu.VMEM((clusters + 1, rows, PANEL), f32)],
        compiler_params=PARAMS,
        cost_estimate=pl.CostEstimate(
            flops=64 * near_count * rows * PANEL * PANEL, bytes_accessed=near_count * 4 * PANEL * PANEL, transcendentals=0),
        name="own",
    )(src_row, tgt_row, far_tgt, field, labels, own_coeffs, far_u, near_blocks)

    late = min(LATE, len(arrived))
    if late < len(arrived):
        total = pl.pallas_call(
            functools.partial(first_target_kernel, depth, used),
            out_shape=shape((sharers, rows, width), f32),
            in_specs=[VMEM] * (2 + len(arrived) - late),
            out_specs=VMEM,
            compiler_params=PARAMS,
            name="target_first",
        )(total, spread, *arrived[:len(arrived) - late])

    def target(steps, dtype, dims, name):
        return pl.pallas_call(
            functools.partial(last_target_kernel, depth, used, late, steps),
            out_shape=[shape(dims, dtype)] * len(steps),
            in_specs=[VMEM] * (2 + late),
            out_specs=[VMEM] * len(steps),
            compiler_params=PARAMS,
            name=name,
        )(total, spread, *arrived[len(arrived) - late:])

    received = []
    if sharers > 1:
        others = target(tuple(range(1, sharers)), bf16, (rows, width), "target_others")
        received = [
            lax.ppermute(other, "tgt", [(t, (t + k) % sharers) for t in range(sharers)])
            for k, other in enumerate(others, 1)
        ]
    (result,) = target((0,), f32, (2, half, width), "target_mine")
    for other in received:
        result = result + other.astype(f32).reshape(result.shape)
    return result


def solution(mesh):
    placed = (
        P(None, "dir", ("groups", "src")),
        P(("groups", "src"), "tgt", None, None, None, None),
        P(("groups", "src"), "tgt", None),
        P(("groups", "src"), "tgt", None),
        P(("groups", "src"), "tgt", None, None, None, None),
        P(("groups", "src"), "tgt", None),
        P(("groups", "src"), "tgt", None),
        P(("groups", "src"), "tgt", None, None, None, None),
        P(("groups", "src"), "tgt", None),
    )
    return jax.shard_map(
        body,
        mesh=mesh,
        in_specs=placed,
        out_specs=P(None, "dir", ("groups", "src", "tgt")),
        check_vma=False,
    )
```
